32 devices in a mesh: rep: 16 (over z, y, core), shard: 2 (over x).
Axes of the slice: x: 2, y: 2, z: 4, core: 2. Of those that a mesh axis runs over, the one named last changes fastest.
Arguments:
- tokens: bfloat16 [4096, 2048], P(('rep', 'shard')), may hold values from -6 to 6
- routes: int32 [4096, 2], P(('rep', 'shard')), may hold values from 0 to 7, all different within a row; in each aligned block of 128 rows (0 to 127, 128 to 255, ...) at most 48 rows name the same one
- route_weight: float32 [4096, 2], P(('rep', 'shard')), may hold values from 0.2 to 1
- w_gate: bfloat16 [8, 2048, 768], P('shard'), may hold values from -0.125 to 0.125
- w_up: bfloat16 [8, 2048, 768], P('shard'), may hold values from -0.125 to 0.125
- w_down: bfloat16 [8, 768, 2048], P('shard'), may hold values from -0.21875 to 0.21875
- pseudo_grad: float32 [16, 192, 2048], P('rep', 'shard'), may hold values from -5400 to 5400
- global_params: float32 [192, 2048], P('shard'), may hold values from -6 to 6
- momentum: float32 [192, 2048], P('shard', 'rep'), may hold values from -3 to 3
- local_params: bfloat16 [16, 192, 2048], P('rep', 'shard'), may hold values from -6 to 6
Outputs:
- moe_out: bfloat16 [4096, 2048], P(('rep', 'shard'))
- momentum_next: float32 [192, 2048], P('shard', 'rep')
- local_next: bfloat16 [16, 192, 2048], P('rep', 'shard')
The draws below stay inside these ranges and needn't reach their ends.
Inputs may be any that keep to these rules, and one draw needn't show every extreme that they name: `routes`: each token names 2 different experts. Within the rows of one device no expert is named by more than 48 rows, and on some device one is named by exactly 48.
All inputs are finite; a program needn't handle non-finite values.
Results may differ from the reference program's by a relative error of at most 0.0057.
Values may be sent and summed in bfloat16 or wider, within the bound.
A program may use at most 128 MiB of HBM per device.

```python
import math
import jax
import jax.numpy as jnp
import numpy as np
from jax import lax

D = 2048
FF_WIN = 768
EXPERTS = 8
TOPK = 2
TOK_DEV = 128
CAP = 48
REPLICAS = 16
TOKENS = 4096
FRAG_ROWS = 192


def draw_pseudo_grad(key, part):
    key = jax.random.fold_in(key, 11)
    key_rows, key_cols, key_own = jax.random.split(key, 3)
    rising = 1.0 + 2.0 * jnp.arange(FRAG_ROWS, dtype=jnp.float32) / max(FRAG_ROWS - 1, 1)
    row_scale = jnp.exp(jax.random.uniform(key_rows, (FRAG_ROWS,), jnp.float32, 0.0, math.log(10.0))) * rising
    col_scale = jnp.exp(jax.random.uniform(key_cols, (D,), jnp.float32, 0.0, math.log(10.0)))
    own_part = jax.random.normal(key_own, (REPLICAS, FRAG_ROWS, D), jnp.float32)
    base = jnp.clip(own_part, -6.0, 6.0)
    return (base * row_scale[None, :, None] * col_scale[None, None, :]).astype(jnp.float32)


def block_scale(own_key, dims, pieces, least, largest):
    def one(dim, parts):
        draws = jax.random.uniform(jax.random.fold_in(jax.random.fold_in(own_key, 6), dim), (parts,), jnp.float32, least / len(pieces), largest / len(pieces))
        return jnp.repeat(jnp.exp(draws), dims[dim] // parts).reshape((-1,) + (1,) * (len(dims) - dim - 1))

    loudness = one(*pieces[0])
    for cut in pieces[1:]:
        loudness = loudness * one(*cut)
    return loudness


def shared_out(key, own, number, rows, amount, top, limit, lean):
    order = jax.random.permutation(key, amount)
    heavy_load, ordinary = shares(amount, rows * top, limit, lean, True), shares(amount, rows * top, limit, lean, False)
    places = jnp.arange(amount)

    def named(tallies, rotation):
        used = int((tallies > 0).sum())
        fixed = max(1, used // 4)
        passed = fixed + (places - fixed + rotation * (used - fixed)) % max(1, amount - fixed)
        return jnp.zeros((amount,), jnp.int32).at[order[jnp.where(places < fixed, places, passed)]].set(jnp.asarray(tallies, jnp.int32))

    tallies = jnp.where(number % 4 == 0, named(heavy_load, number // 4), named(ordinary, number - number // 4 - 1))
    mixed = jax.random.permutation(jax.random.fold_in(own, 3), amount)
    giver, receiver = mixed[0:amount // 2 * 2:2], mixed[1:amount // 2 * 2:2]
    room = jnp.minimum(tallies[giver] - 1, limit - tallies[receiver]) // 2
    room = jnp.where((giver == order[0]) | (receiver == order[0]) | (tallies[receiver] == 0), 0, jnp.maximum(room, 0))
    passed = jax.random.randint(jax.random.fold_in(own, 4), (amount // 2,), 0, 1 << 20) % (room + 1)
    tallies = tallies.at[giver].add(-passed).at[receiver].add(passed)
    labels = jnp.searchsorted(jnp.cumsum(tallies), jnp.arange(rows * top), side="right").astype(jnp.int32)
    table = labels.reshape(top, rows).T
    table = table[jax.random.permutation(jax.random.fold_in(own, 1), rows)]
    rotation = jax.random.randint(jax.random.fold_in(own, 2), (rows, 1), 0, top)
    return jnp.take_along_axis(table, (jnp.arange(top)[None, :] + rotation) % top, axis=1)


def shares(amount, total, limit, skew, full):
    portions = [(1 << 20) // math.isqrt(rank ** skew) + 1 for rank in range(1, amount + 1)]
    largest = limit if full else min(limit, max(-(-total // amount), total * portions[0] // sum(portions)))
    least = 1 if total - largest >= amount - 1 else 0
    given, rest = [largest] + [least] * (amount - 1), total - largest - least * (amount - 1)
    while rest > 0:
        candidates = [i for i in range(1, amount) if given[i] < largest] or [i for i in range(1, amount) if given[i] < limit]
        mass, budget = sum([portions[i] for i in candidates]), rest
        for i in candidates:
            extra = min(limit - given[i], max(1, budget * portions[i] // mass), rest)
            given[i] = given[i] + extra
            rest = rest - extra
    return np.array(given)


def centred(rng, dims, spread, limit, shards=(), held_as=jnp.bfloat16):
    loudness = block_scale(rng, dims, shards, -0.22, 0.18) if shards else 1.0
    values = jax.random.normal(rng, dims, jnp.float32) * spread * loudness
    return jnp.minimum(jnp.maximum(values, -limit), limit).astype(held_as)


def setup_inputs(seed: int = 0) -> dict:
    seeds = jax.random.split(jax.random.key(seed), 11)
    tokens = centred(seeds[0], (TOKENS, D), 1.0, 6.0, ((0, 32),))
    routes_keys = jax.random.split(jax.random.fold_in(seeds[1], 1), TOKENS // TOK_DEV)
    routes_turns = jax.random.permutation(jax.random.fold_in(seeds[1], 3), TOKENS // TOK_DEV)
    routes = jax.vmap(lambda own, number: shared_out(jax.random.fold_in(seeds[1], 2), own, number, TOK_DEV, EXPERTS, TOPK, CAP, 1))(routes_keys, routes_turns).reshape((TOKENS, TOPK))
    route_weight = jnp.clip(0.2 + 0.8 * jax.random.uniform(seeds[2], (TOKENS, TOPK), jnp.float32) ** block_scale(seeds[2], (TOKENS, TOPK), ((0, 32),), -0.2, 0.2), 0.2, 1.0)
    w_gate = centred(seeds[3], (EXPERTS, D, FF_WIN), D ** -0.5, 0.125, ((0, 2),))
    w_up = centred(seeds[4], (EXPERTS, D, FF_WIN), D ** -0.5, 0.125, ((0, 2),))
    w_down = centred(seeds[5], (EXPERTS, FF_WIN, D), FF_WIN ** -0.5, 0.21875, ((0, 2),))
    pseudo_grad = draw_pseudo_grad(jax.random.fold_in(seeds[10], 71), 0)
    global_params = centred(seeds[7], (FRAG_ROWS, D), 1.0, 6.0, ((0, 2),), jnp.float32)
    momentum = centred(seeds[8], (FRAG_ROWS, D), 0.5, 3.0, ((0, 2), (1, 16)), jnp.float32)
    local_params = centred(seeds[9], (REPLICAS, FRAG_ROWS, D), 1.0, 6.0, ((0, 16), (1, 2)))
    return {"tokens": tokens, "routes": routes, "route_weight": route_weight, "w_gate": w_gate, "w_up": w_up, "w_down": w_down, "pseudo_grad": pseudo_grad, "global_params": global_params, "momentum": momentum, "local_params": local_params}


outer_momentum = 0.9
outer_rate = 0.7
merge_weight = 0.5
clip_epsilon = 1e-06

def slot_table(flat_routes):
    one_hot = (flat_routes[:, None] == jnp.arange(EXPERTS, dtype=jnp.int32)[None, :]).astype(jnp.int32)
    earlier = jnp.cumsum(one_hot, axis=0) - one_hot
    position = lax.optimization_barrier(jnp.sum(earlier * one_hot, axis=1))
    return (flat_routes * CAP + position).astype(jnp.int32)

def expert_apply(operands):
    expert_rows, gate_mat, up_mat, down_mat = operands
    gate = jnp.dot(expert_rows, gate_mat, preferred_element_type=jnp.float32)
    upward = jnp.dot(expert_rows, up_mat, preferred_element_type=jnp.float32)
    hidden = (jax.nn.silu(gate) * upward).astype(jnp.bfloat16)
    return jnp.dot(hidden, down_mat, preferred_element_type=jnp.float32).astype(jnp.bfloat16)

def reference(tokens, routes, route_weight, w_gate, w_up, w_down, pseudo_grad, global_params, momentum, local_params):
    blocks = TOKENS // TOK_DEV
    feat_width = tokens.shape[1]
    block_tokens = tokens.reshape(blocks, TOK_DEV, feat_width)
    block_routes = routes.reshape(blocks, TOK_DEV * TOPK)
    slot_index = jax.vmap(slot_table)(block_routes)
    sources = jnp.repeat(block_tokens, TOPK, axis=1)
    empty = jnp.zeros((blocks, EXPERTS * CAP, feat_width), tokens.dtype)
    buffer = jax.vmap(lambda base, where, values: base.at[where].set(values))(empty, slot_index, sources)
    per_expert = buffer.reshape(blocks, EXPERTS, CAP, feat_width).transpose(1, 0, 2, 3).reshape(EXPERTS, blocks * CAP, feat_width)
    expert_out = lax.map(expert_apply, (per_expert, w_gate, w_up, w_down))
    returned = expert_out.reshape(EXPERTS, blocks, CAP, feat_width).transpose(1, 0, 2, 3).reshape(blocks, EXPERTS * CAP, feat_width)
    picked = jax.vmap(lambda table, where: table[where])(returned, slot_index)
    picked = picked.reshape(blocks, TOK_DEV, TOPK, feat_width).astype(jnp.float32)
    weights = route_weight.reshape(blocks, TOK_DEV, TOPK, 1)
    moe_out = lax.optimization_barrier(jnp.sum(weights * picked, axis=2)).reshape(TOKENS, feat_width).astype(jnp.bfloat16)
    mean_delta = lax.optimization_barrier(jnp.sum(pseudo_grad, axis=0)) / REPLICAS
    mean_square = jnp.mean(mean_delta * mean_delta)
    clip_factor = jnp.minimum(1.0, lax.rsqrt(mean_square + clip_epsilon))
    clipped = clip_factor * mean_delta
    momentum_next = outer_momentum * momentum + clipped
    global_next = global_params - outer_rate * (outer_momentum * momentum_next + clipped)
    local_next = (merge_weight * local_params.astype(jnp.float32) + (1.0 - merge_weight) * global_next[None]).astype(jnp.bfloat16)
    return (moe_out, momentum_next, local_next)
```

```python
import functools

import jax
import jax.numpy as jnp
from jax import lax
from jax.experimental import pallas as pl
from jax.experimental.pallas import tpu as pltpu
from jax.sharding import PartitionSpec as P

outer_momentum = 0.9
outer_rate = 0.7
merge_weight = 0.5
clip_epsilon = 1e-06


def slot_table(flat_routes, experts, capacity):
    one_hot = (flat_routes[:, None] == jnp.arange(experts, dtype=jnp.int32)[None, :]).astype(
        jnp.int32
    )
    earlier = jnp.cumsum(one_hot, axis=0) - one_hot
    position = jnp.sum(earlier * one_hot, axis=1)
    return flat_routes * capacity + position


def local(
    tokens,
    routes,
    route_weight,
    w_gate,
    w_up,
    w_down,
    pseudo_grad,
    global_params,
    momentum,
    local_params,
):
    tok_rows, feat_width = tokens.shape
    top_count = routes.shape[1]
    local_experts = w_gate.shape[0]
    experts = local_experts * lax.axis_size("shard")
    capacity = tok_rows * 3 // 8
    slot_index = slot_table(routes.reshape(-1), experts, capacity)
    matches = (
        jnp.arange(experts * capacity, dtype=jnp.int32)[:, None] == slot_index[None, :]
    ).astype(jnp.bfloat16)
    placement = jnp.sum(matches.reshape(experts * capacity, tok_rows, top_count), axis=2)
    outgoing = jnp.dot(placement, tokens, preferred_element_type=jnp.float32).astype(jnp.bfloat16)
    outgoing = outgoing.reshape(experts, capacity, feat_width)
    received = lax.all_to_all(outgoing, "shard", split_axis=0, concat_axis=0, tiled=True)
    total_rows = received.shape[0]
    slot_count = received.shape[1]
    grouped = received.reshape(total_rows // local_experts, local_experts, slot_count, feat_width)
    gate = jnp.einsum("spcd,pdf->spcf", grouped, w_gate, preferred_element_type=jnp.float32)
    upward = jnp.einsum("spcd,pdf->spcf", grouped, w_up, preferred_element_type=jnp.float32)
    hidden = (jax.nn.silu(gate) * upward).astype(jnp.bfloat16)
    result = jnp.einsum(
        "spcf,pfd->spcd", hidden, w_down, preferred_element_type=jnp.float32
    ).astype(jnp.bfloat16)
    result = result.reshape(total_rows, slot_count, feat_width)
    returned = lax.all_to_all(result, "shard", split_axis=0, concat_axis=0, tiled=True)
    picked = returned.reshape(experts * capacity, feat_width)[slot_index]
    picked = picked.reshape(tok_rows, top_count, feat_width).astype(jnp.float32)
    moe_out = jnp.sum(route_weight[:, :, None] * picked, axis=1).astype(jnp.bfloat16)
    replicas = lax.axis_size("rep")
    own_delta = pseudo_grad[0]
    frag_rows = own_delta.shape[0]
    entry_count = float(frag_rows * lax.axis_size("shard") * feat_width)
    col_width = momentum.shape[1]
    col_start = lax.axis_index("rep") * col_width
    delta_total = lax.psum(own_delta, "rep")
    mean_delta = delta_total / replicas
    square_sum = lax.psum(jnp.sum(mean_delta * mean_delta), "shard")
    clip_factor = jnp.minimum(1.0, lax.rsqrt(square_sum / entry_count + clip_epsilon))
    clipped = clip_factor * mean_delta
    full_momentum = lax.all_gather(momentum, "rep", axis=1, tiled=True)
    momentum_full = outer_momentum * full_momentum + clipped
    global_next = global_params - outer_rate * (outer_momentum * momentum_full + clipped)
    momentum_next = lax.dynamic_slice_in_dim(momentum_full, col_start, col_width, 1)
    local_next = (
        merge_weight * local_params.astype(jnp.float32) + (1.0 - merge_weight) * global_next[None]
    ).astype(jnp.bfloat16)
    return (moe_out, momentum_next, local_next)


LANES = 128
MESH = pl.DeviceIdType.MESH


def kernel(
    reps,
    tokens,
    routes,
    route_weight,
    w_gate,
    w_up,
    w_down,
    pseudo_grad,
    global_params,
    momentum,
    local_params,
    moe_out,
    momentum_next,
    local_next,
    gate_s,
    up_s,
    down_s,
    own_tok,
    far_tok,
    mix_own,
    mix_send,
    mix_far,
    col_own,
    col_far,
    hid_own,
    hid_far,
    sum_own,
    back_send,
    back,
    out_s,
    grad_own,
    grad_sib,
    grad_sum,
    grad_far,
    sq_own,
    sq_far,
    sq_chip,
    sq_sib,
    sq_half,
    sq_other,
    mom_s,
    glob_s,
    loc_s,
    upd,
    mom_out,
    loc_out,
    w_sem,
    in_sem,
    out_sem,
    g_sem,
    tok_sem,
    mix_sem,
    back_sem,
    sib_sem,
    far_sem,
    sq_sem,
    one_sem,
    upd_sem,
    fwd_sem,
):
    experts = w_gate.shape[0]
    rows, width = tokens.shape
    hidden = w_gate.shape[2]
    chunks, tiles, chunk_rows, tile_cols = back.shape
    frag_rows = momentum.shape[0]
    chips = reps // 2

    rep = lax.axis_index("rep")
    shard = lax.axis_index("shard")
    chip = rep // 2
    core = rep % 2
    partner = (rep, 1 - shard)
    sibling = (chip * 2 + 1 - core, shard)

    def peer(step):
        return (((chip + step) % chips) * 2 + core, shard)

    def columns(index):
        return pl.ds(pl.multiple_of(index * LANES, LANES), LANES)

    weights = []
    for e in range(experts):
        weights.append(pltpu.make_async_copy(w_gate.at[e], gate_s.at[e], w_sem.at[0, e]))
        weights.append(pltpu.make_async_copy(w_up.at[e], up_s.at[e], w_sem.at[1, e]))
    for e in range(experts):
        weights.append(
            pltpu.make_async_copy(w_down.at[e], down_s.at[pl.ds(e * hidden, hidden)], w_sem.at[2, e])
        )
    load_tok = pltpu.make_async_copy(tokens, own_tok, in_sem.at[0])
    load_glob = pltpu.make_async_copy(global_params, glob_s, in_sem.at[1])
    load_mom = pltpu.make_async_copy(momentum, mom_s, in_sem.at[2])
    load_loc = pltpu.make_async_copy(local_params.at[0], loc_s, in_sem.at[3])
    load_grad = [
        pltpu.make_async_copy(
            pseudo_grad.at[0, :, columns(2 * k + core)], grad_own.at[k], g_sem.at[k]
        )
        for k in range(chips)
    ]

    load_tok.start()
    for copy in weights[:2]:
        copy.start()
    for copy in load_grad:
        copy.start()

    ids = lax.broadcasted_iota(jnp.int32, (8, rows), 0)
    mix = jnp.zeros((8, rows), jnp.float32)
    for k in range(routes.shape[0]):
        mix = mix + jnp.where(ids == routes[k : k + 1, :], route_weight[k : k + 1, :], 0.0)
    mix_send[...] = mix
    rest = jnp.zeros((LANES - 8, rows), jnp.float32)
    mix_own[...] = jnp.concatenate([mix, rest], axis=0).T

    barrier = pltpu.get_barrier_semaphore()
    for device in [partner, sibling] + [peer(j) for j in range(1, chips)]:
        pl.semaphore_signal(barrier, inc=1, device_id=device, device_id_type=MESH)
    pl.semaphore_wait(barrier, 1 + chips)

    def remote(src, dst, sems, index, device):
        return pltpu.make_async_remote_copy(
            src_ref=src,
            dst_ref=dst,
            send_sem=sems.at[(0,) + index],
            recv_sem=sems.at[(1,) + index],
            device_id=device,
            device_id_type=MESH,
        )

    send_mix = remote(mix_send, mix_far, mix_sem, (0,), partner)
    send_mix.start()
    send_tok = []
    for c in range(chunks):
        part = pl.ds(c * chunk_rows, chunk_rows)
        send_tok.append(remote(tokens.at[part], far_tok.at[part], tok_sem, (c,), partner))
        send_tok[c].start()
    send_sib = []
    for k in range(chips):
        send_sib.append(
            remote(
                pseudo_grad.at[0, :, columns(2 * k + 1 - core)], grad_sib.at[k], sib_sem, (k,), sibling
            )
        )
        send_sib[k].start()
    for copy in weights[2:]:
        copy.start()
    load_loc.start()
    load_glob.start()
    load_mom.start()

    def gate_up(tok, part, col, hid, e):
        tok_part = tok[part, :]
        scale = col[part, pl.ds(0, 1)]
        for f in range(0, hidden, 256):
            gate = jnp.dot(tok_part, gate_s[e, :, f : f + 256], preferred_element_type=jnp.float32)
            upward = jnp.dot(tok_part, up_s[e, :, f : f + 256], preferred_element_type=jnp.float32)
            value = gate / (1.0 + jnp.exp(-gate)) * upward * scale
            hid[part, pl.ds(pl.multiple_of(e * hidden + f, LANES), 256)] = value.astype(jnp.bfloat16)

    def pick(mix_ref, col, e):
        lanes = lax.broadcasted_iota(jnp.int32, (rows, LANES), 1)
        chosen = jnp.where(lanes == shard * experts + e, mix_ref[...], 0.0)
        col[...] = jnp.broadcast_to(jnp.sum(chosen, axis=1, keepdims=True), (rows, LANES))

    whole = pl.ds(0, rows)

    def own_step(e, carry):
        pltpu.make_async_copy(w_gate.at[e], gate_s.at[e], w_sem.at[0, e]).wait()
        pltpu.make_async_copy(w_up.at[e], up_s.at[e], w_sem.at[1, e]).wait()
        pick(mix_own, col_own, e)
        gate_up(own_tok, whole, col_own, hid_own, e)
        return carry

    load_tok.wait()
    lax.fori_loop(0, experts // 2, own_step, 0)

    for copy in load_grad:
        copy.wait()
    for copy in send_sib:
        copy.wait_recv()

    def chip_sum(k, carry):
        grad_sum[k] = grad_own[k] + grad_sib[k]
        return carry

    lax.fori_loop(0, chips, chip_sum, 0)
    send_far = []
    for j in range(1, chips):
        send_far.append(
            remote(grad_sum.at[(chip + j) % chips], grad_far.at[j - 1], far_sem, (j - 1,), peer(j))
        )
        send_far[j - 1].start()

    lax.fori_loop(experts // 2, experts, own_step, 0)

    send_mix.wait_recv()
    mix_own[...] = jnp.concatenate([mix_far[...], rest], axis=0).T

    def far_rows(c):
        part = pl.ds(c * chunk_rows, chunk_rows)
        send_tok[c].wait_recv()

        def far_step(e, carry):
            pick(mix_own, col_far, e)
            gate_up(far_tok, part, col_far, hid_far, e)
            return carry

        lax.fori_loop(0, experts, far_step, 0)

    def down(hid_part, t):
        return jnp.dot(
            hid_part,
            down_s[:, t * tile_cols : (t + 1) * tile_cols],
            preferred_element_type=jnp.float32,
        )

    send_back = []

    def far_down(c):
        part = pl.ds(c * chunk_rows, chunk_rows)
        for t in range(tiles):
            back_send[c, t] = down(hid_far[part, :], t).astype(jnp.bfloat16)
            copy = remote(back_send.at[c, t], back.at[c, t], back_sem, (c, t), partner)
            copy.start()
            send_back.append(copy)

    far_rows(0)
    for copy in weights[2 * experts :]:
        copy.wait()
    far_down(0)
    for c in range(1, chunks):
        far_rows(c)
        far_down(c)

    for copy in send_far:
        copy.wait_recv()
    total = grad_sum[chip]
    for j in range(1, chips):
        total = total + grad_far[j - 1]
    mean = total / reps
    squares = mean * mean
    square = squares[0:8]
    for i in range(8, frag_rows, 8):
        square = square + squares[i : i + 8]
    sq_own[...] = square
    send_sq = []
    for j in range(1, chips):
        send_sq.append(remote(sq_own, sq_far.at[j - 1], sq_sem, (j - 1,), peer(j)))
        send_sq[j - 1].start()

    for t in range(tiles):
        sum_own[:, t * tile_cols : (t + 1) * tile_cols] = down(hid_own[...], t)

    for copy in send_sq:
        copy.wait_recv()
    square = sq_own[...]
    for j in range(1, chips):
        square = square + sq_far[j - 1]
    sq_chip[...] = square
    to_sib = remote(sq_chip, sq_sib, one_sem, (0,), sibling)
    to_sib.start()
    to_sib.wait_recv()
    sq_half[...] = sq_chip[...] + sq_sib[...]
    to_other = remote(sq_half, sq_other, one_sem, (1,), partner)
    to_other.start()
    to_other.wait_recv()
    entries = float(frag_rows * 2 * width)
    square_sum = jnp.sum(sq_half[...] + sq_other[...])
    clip_factor = jnp.minimum(1.0, lax.rsqrt(square_sum / entries + clip_epsilon))
    clipped = clip_factor * mean
    load_mom.wait()
    fresh = outer_momentum * mom_s[...] + clipped
    mom_out[...] = fresh
    store_mom = pltpu.make_async_copy(mom_out, momentum_next, out_sem.at[0])
    store_mom.start()
    upd[rep] = (outer_rate * (outer_momentum * fresh + clipped)).astype(jnp.bfloat16)

    send_upd = []
    for j in range(1, chips):
        send_upd.append(remote(upd.at[rep], upd.at[rep], upd_sem, (j - 1,), peer(j)))
        send_upd[j - 1].start()
    forward = [remote(upd.at[rep], upd.at[rep], fwd_sem, (0,), sibling)]
    forward[0].start()
    load_loc.wait()
    load_glob.wait()

    def merge(index):
        cols = columns(index)
        later = glob_s[:, cols] - upd[index].astype(jnp.float32)
        merged = merge_weight * loc_s[:, cols].astype(jnp.float32) + (1.0 - merge_weight) * later
        loc_out[:, cols] = merged.astype(jnp.bfloat16)

    merge(rep)
    for j in range(1, chips):
        send_upd[j - 1].wait_recv()
        came = ((chip - j + chips) % chips) * 2 + core
        forward.append(remote(upd.at[came], upd.at[came], fwd_sem, (j,), sibling))
        forward[j].start()
        merge(came)
    for j in range(chips):
        forward[j].wait_recv()
        merge(((chip - j + chips) % chips) * 2 + 1 - core)
    store_loc = pltpu.make_async_copy(loc_out, local_next.at[0], out_sem.at[1])
    store_loc.start()

    stores = []
    for c in range(chunks):
        part = pl.ds(c * chunk_rows, chunk_rows)
        for t in range(tiles):
            send_back[c * tiles + t].wait_recv()
            cols = pl.ds(t * tile_cols, tile_cols)
            out_s[part, cols] = (sum_own[part, cols] + back[c, t].astype(jnp.float32)).astype(
                jnp.bfloat16
            )
        stores.append(pltpu.make_async_copy(out_s.at[part], moe_out.at[part], out_sem.at[2 + c]))
        stores[c].start()

    for copy in [send_mix, to_sib, to_other] + send_tok + send_sib + send_far + send_sq + send_back:
        copy.wait_send()
    for copy in send_upd + forward:
        copy.wait_send()
    for copy in stores + [store_mom, store_loc]:
        copy.wait()


def fused(
    reps,
    tokens,
    routes,
    route_weight,
    w_gate,
    w_up,
    w_down,
    pseudo_grad,
    global_params,
    momentum,
    local_params,
):
    rows, width = tokens.shape
    experts, _, hidden = w_gate.shape
    frag_rows = momentum.shape[0]
    chips = reps // 2
    chunks, tiles = 2, 4
    f32, bf16 = jnp.float32, jnp.bfloat16
    anywhere = pl.BlockSpec(memory_space=pl.ANY)
    in_vmem = pl.BlockSpec(memory_space=pltpu.VMEM)
    dma = pltpu.SemaphoreType.DMA
    block = (frag_rows, LANES)
    returned = (chunks, tiles, rows // chunks, width // tiles)
    return pl.pallas_call(
        functools.partial(kernel, reps),
        out_shape=(
            jax.ShapeDtypeStruct(tokens.shape, tokens.dtype),
            jax.ShapeDtypeStruct(momentum.shape, momentum.dtype),
            jax.ShapeDtypeStruct(local_params.shape, local_params.dtype),
        ),
        in_specs=[anywhere, in_vmem, in_vmem] + [anywhere] * 7,
        out_specs=(anywhere,) * 3,
        scratch_shapes=[
            pltpu.VMEM(w_gate.shape, bf16),
            pltpu.VMEM(w_up.shape, bf16),
            pltpu.VMEM((experts * hidden, width), bf16),
            pltpu.VMEM(tokens.shape, bf16),
            pltpu.VMEM(tokens.shape, bf16),
            pltpu.VMEM((rows, LANES), f32),
            pltpu.VMEM((8, rows), f32),
            pltpu.VMEM((8, rows), f32),
            pltpu.VMEM((rows, LANES), f32),
            pltpu.VMEM((rows, LANES), f32),
            pltpu.VMEM((rows, experts * hidden), bf16),
            pltpu.VMEM((rows, experts * hidden), bf16),
            pltpu.VMEM((rows, width), f32),
            pltpu.VMEM(returned, bf16),
            pltpu.VMEM(returned, bf16),
            pltpu.VMEM(tokens.shape, bf16),
            pltpu.VMEM((chips,) + block, f32),
            pltpu.VMEM((chips,) + block, f32),
            pltpu.VMEM((chips,) + block, f32),
            pltpu.VMEM((chips - 1,) + block, f32),
            pltpu.VMEM((8, LANES), f32),
            pltpu.VMEM((chips - 1, 8, LANES), f32),
            pltpu.VMEM((8, LANES), f32),
            pltpu.VMEM((8, LANES), f32),
            pltpu.VMEM((8, LANES), f32),
            pltpu.VMEM((8, LANES), f32),
            pltpu.VMEM(block, f32),
            pltpu.VMEM((frag_rows, width), f32),
            pltpu.VMEM((frag_rows, width), bf16),
            pltpu.VMEM((reps,) + block, bf16),
            pltpu.VMEM(block, f32),
            pltpu.VMEM((frag_rows, width), bf16),
            dma((3, experts)),
            dma((4,)),
            dma((2 + chunks,)),
            dma((chips,)),
            dma((2, chunks)),
            dma((2, 1)),
            dma((2, chunks, tiles)),
            dma((2, chips)),
            dma((2, chips - 1)),
            dma((2, chips - 1)),
            dma((2, 2)),
            dma((2, chips - 1)),
            dma((2, chips)),
        ],
        compiler_params=pltpu.CompilerParams(
            collective_id=0, has_side_effects=True, vmem_limit_bytes=56 * 1024 * 1024
        ),
        cost_estimate=pl.CostEstimate(
            flops=12 * rows * experts * hidden * width,
            bytes_accessed=6 * experts * hidden * width,
            transcendentals=0,
        ),
    )(
        tokens,
        routes.T,
        route_weight.T,
        w_gate,
        w_up,
        w_down,
        pseudo_grad,
        global_params,
        momentum,
        local_params,
    )


def solution(mesh):
    in_specs = (
        P(("rep", "shard"), None),
        P(("rep", "shard"), None),
        P(("rep", "shard"), None),
        P("shard", None, None),
        P("shard", None, None),
        P("shard", None, None),
        P("rep", "shard", None),
        P("shard", None),
        P("shard", "rep"),
        P("rep", "shard", None),
    )
    out_specs = (P(("rep", "shard"), None), P("shard", "rep"), P("rep", "shard", None))
    reps, shards = mesh.shape["rep"], mesh.shape["shard"]

    def step(*arrays):
        tokens, w_gate, momentum = arrays[0], arrays[3], arrays[8]
        pairs = shards == 2 and reps % 2 == 0 and reps >= 4
        aligned = momentum.shape[1] == LANES and tokens.shape[0] == LANES
        if pairs and aligned and w_gate.shape[0] * shards == 8:
            return fused(reps, *arrays)
        return local(*arrays)

    return jax.shard_map(step, mesh=mesh, in_specs=in_specs, out_specs=out_specs, check_vma=False)
```

```python
import functools

import jax
import jax.numpy as jnp
from jax import lax
from jax.experimental import pallas as pl
from jax.experimental.pallas import tpu as pltpu
from jax.sharding import PartitionSpec as P

outer_momentum = 0.9
outer_rate = 0.7
merge_weight = 0.5
clip_epsilon = 1e-06


def slot_table(flat_routes, experts, capacity):
    one_hot = (flat_routes[:, None] == jnp.arange(experts, dtype=jnp.int32)[None, :]).astype(
        jnp.int32
    )
    earlier = jnp.cumsum(one_hot, axis=0) - one_hot
    position = jnp.sum(earlier * one_hot, axis=1)
    return flat_routes * capacity + position


def local(
    tokens,
    routes,
    route_weight,
    w_gate,
    w_up,
    w_down,
    pseudo_grad,
    global_params,
    momentum,
    local_params,
):
    tok_rows, feat_width = tokens.shape
    top_count = routes.shape[1]
    local_experts = w_gate.shape[0]
    experts = local_experts * lax.axis_size("shard")
    capacity = tok_rows * 3 // 8
    slot_index = slot_table(routes.reshape(-1), experts, capacity)
    matches = (
        jnp.arange(experts * capacity, dtype=jnp.int32)[:, None] == slot_index[None, :]
    ).astype(jnp.bfloat16)
    placement = jnp.sum(matches.reshape(experts * capacity, tok_rows, top_count), axis=2)
    outgoing = jnp.dot(placement, tokens, preferred_element_type=jnp.float32).astype(jnp.bfloat16)
    outgoing = outgoing.reshape(experts, capacity, feat_width)
    received = lax.all_to_all(outgoing, "shard", split_axis=0, concat_axis=0, tiled=True)
    total_rows = received.shape[0]
    slot_count = received.shape[1]
    grouped = received.reshape(total_rows // local_experts, local_experts, slot_count, feat_width)
    gate = jnp.einsum("spcd,pdf->spcf", grouped, w_gate, preferred_element_type=jnp.float32)
    upward = jnp.einsum("spcd,pdf->spcf", grouped, w_up, preferred_element_type=jnp.float32)
    hidden = (jax.nn.silu(gate) * upward).astype(jnp.bfloat16)
    result = jnp.einsum(
        "spcf,pfd->spcd", hidden, w_down, preferred_element_type=jnp.float32
    ).astype(jnp.bfloat16)
    result = result.reshape(total_rows, slot_count, feat_width)
    returned = lax.all_to_all(result, "shard", split_axis=0, concat_axis=0, tiled=True)
    picked = returned.reshape(experts * capacity, feat_width)[slot_index]
    picked = picked.reshape(tok_rows, top_count, feat_width).astype(jnp.float32)
    moe_out = jnp.sum(route_weight[:, :, None] * picked, axis=1).astype(jnp.bfloat16)
    replicas = lax.axis_size("rep")
    own_delta = pseudo_grad[0]
    frag_rows = own_delta.shape[0]
    entry_count = float(frag_rows * lax.axis_size("shard") * feat_width)
    col_width = momentum.shape[1]
    col_start = lax.axis_index("rep") * col_width
    delta_total = lax.psum(own_delta, "rep")
    mean_delta = delta_total / replicas
    square_sum = lax.psum(jnp.sum(mean_delta * mean_delta), "shard")
    clip_factor = jnp.minimum(1.0, lax.rsqrt(square_sum / entry_count + clip_epsilon))
    clipped = clip_factor * mean_delta
    full_momentum = lax.all_gather(momentum, "rep", axis=1, tiled=True)
    momentum_full = outer_momentum * full_momentum + clipped
    global_next = global_params - outer_rate * (outer_momentum * momentum_full + clipped)
    momentum_next = lax.dynamic_slice_in_dim(momentum_full, col_start, col_width, 1)
    local_next = (
        merge_weight * local_params.astype(jnp.float32) + (1.0 - merge_weight) * global_next[None]
    ).astype(jnp.bfloat16)
    return (moe_out, momentum_next, local_next)


LANES = 128
MESH = pl.DeviceIdType.MESH


def kernel(
    reps,
    tokens,
    routes,
    route_weight,
    w_gate,
    w_up,
    w_down,
    pseudo_grad,
    global_params,
    momentum,
    local_params,
    moe_out,
    momentum_next,
    local_next,
    gate_s,
    up_s,
    down_s,
    own_tok,
    far_tok,
    mix_own,
    mix_send,
    mix_far,
    mix_got,
    col_own,
    col_far,
    hid_own,
    hid_far,
    sum_own,
    back_send,
    back,
    out_s,
    grad_own,
    grad_sib,
    grad_sum,
    grad_far,
    sq_own,
    sq_far,
    sq_chip,
    sq_sib,
    sq_half,
    sq_other,
    mean_s,
    mom_s,
    glob_s,
    loc_s,
    upd,
    mom_out,
    loc_out,
    w_sem,
    in_sem,
    out_sem,
    g_sem,
    tok_sem,
    mix_sem,
    back_sem,
    sib_sem,
    far_sem,
    sq_sem,
    one_sem,
    mom_sem,
    upd_sem,
    fwd_sem,
):
    experts = w_gate.shape[0]
    rows, width = tokens.shape
    hidden = w_gate.shape[2]
    chunks, tiles, chunk_rows, tile_cols = back.shape
    frag_rows = momentum.shape[0]
    chips = reps // 2

    rep = lax.axis_index("rep")
    shard = lax.axis_index("shard")
    chip = rep // 2
    core = rep % 2
    partner = (rep, 1 - shard)
    sibling = (chip * 2 + 1 - core, shard)

    def peer(step):
        return (((chip + step) % chips) * 2 + core, shard)

    def columns(index):
        return pl.ds(pl.multiple_of(index * LANES, LANES), LANES)

    weights = []
    for e in range(experts):
        weights.append(pltpu.make_async_copy(w_gate.at[e], gate_s.at[e], w_sem.at[0, e]))
        weights.append(pltpu.make_async_copy(w_up.at[e], up_s.at[e], w_sem.at[1, e]))
    for e in range(experts):
        weights.append(
            pltpu.make_async_copy(w_down.at[e], down_s.at[pl.ds(e * hidden, hidden)], w_sem.at[2, e])
        )
    load_tok = pltpu.make_async_copy(tokens, own_tok, in_sem.at[0])
    load_glob = pltpu.make_async_copy(global_params, glob_s, in_sem.at[1])
    load_mom = pltpu.make_async_copy(momentum, mom_s, in_sem.at[2])
    load_loc = pltpu.make_async_copy(local_params.at[0], loc_s, in_sem.at[3])
    load_grad = [
        pltpu.make_async_copy(
            pseudo_grad.at[0, :, columns(2 * k + core)], grad_own.at[k], g_sem.at[k]
        )
        for k in range(chips)
    ]

    load_mom.start()
    load_tok.start()
    for copy in weights[:2]:
        copy.start()
    for copy in load_grad:
        copy.start()

    ids = lax.broadcasted_iota(jnp.int32, (8, rows), 0)
    mix = jnp.zeros((8, rows), jnp.float32)
    for k in range(routes.shape[0]):
        mix = mix + jnp.where(ids == routes[k : k + 1, :], route_weight[k : k + 1, :], 0.0)
    mix_send[...] = mix
    rest = jnp.zeros((LANES - 8, rows), jnp.float32)
    mix_own[...] = jnp.concatenate([mix, rest], axis=0).T

    barrier = pltpu.get_barrier_semaphore()
    for device in [partner, sibling] + [peer(j) for j in range(1, chips)]:
        pl.semaphore_signal(barrier, inc=1, device_id=device, device_id_type=MESH)
    pl.semaphore_wait(barrier, 1 + chips)

    def remote(src, dst, sems, index, device):
        return pltpu.make_async_remote_copy(
            src_ref=src,
            dst_ref=dst,
            send_sem=sems.at[(0,) + index],
            recv_sem=sems.at[(1,) + index],
            device_id=device,
            device_id_type=MESH,
        )

    send_mix = remote(mix_send, mix_far, mix_sem, (0,), partner)
    send_mix.start()
    send_tok = []
    for c in range(chunks):
        part = pl.ds(c * chunk_rows, chunk_rows)
        send_tok.append(remote(tokens.at[part], far_tok.at[part], tok_sem, (c,), partner))
        send_tok[c].start()
    send_sib = []
    for k in range(chips):
        send_sib.append(
            remote(
                pseudo_grad.at[0, :, columns(2 * k + 1 - core)], grad_sib.at[k], sib_sem, (k,), sibling
            )
        )
        send_sib[k].start()
    load_mom.wait()
    upd[rep, 0] = mom_s[...].astype(jnp.bfloat16)
    send_mom = []
    for j in range(1, chips):
        send_mom.append(remote(upd.at[rep, 0], upd.at[rep, 0], mom_sem, (j - 1,), peer(j)))
        send_mom[j - 1].start()
    for copy in weights[2:]:
        copy.start()
    load_loc.start()
    load_glob.start()

    def gate_up(tok, part, col, hid, e):
        tok_part = tok[part, :]
        scale = col[part, pl.ds(0, 1)]
        for f in range(0, hidden, 256):
            gate = jnp.dot(tok_part, gate_s[e, :, f : f + 256], preferred_element_type=jnp.float32)
            upward = jnp.dot(tok_part, up_s[e, :, f : f + 256], preferred_element_type=jnp.float32)
            value = gate / (1.0 + jnp.exp(-gate)) * upward * scale
            hid[part, pl.ds(pl.multiple_of(e * hidden + f, LANES), 256)] = value.astype(jnp.bfloat16)

    def pick(mix_ref, col, e):
        lanes = lax.broadcasted_iota(jnp.int32, (rows, LANES), 1)
        chosen = jnp.where(lanes == shard * experts + e, mix_ref[...], 0.0)
        col[...] = jnp.broadcast_to(jnp.sum(chosen, axis=1, keepdims=True), (rows, LANES))

    whole = pl.ds(0, rows)

    def own_rows(e):
        pick(mix_own, col_own, e)
        gate_up(own_tok, whole, col_own, hid_own, e)

    def own_step(e, carry):
        pltpu.make_async_copy(w_gate.at[e], gate_s.at[e], w_sem.at[0, e]).wait()
        pltpu.make_async_copy(w_up.at[e], up_s.at[e], w_sem.at[1, e]).wait()
        own_rows(e)
        return carry

    load_tok.wait()
    lax.fori_loop(0, 1, own_step, 0)

    for copy in load_grad:
        copy.wait()
    for copy in send_sib:
        copy.wait_recv()

    def chip_sum(k, carry):
        grad_sum[k] = grad_own[k] + grad_sib[k]
        return carry

    lax.fori_loop(0, chips, chip_sum, 0)
    send_far = []
    for j in range(1, chips):
        send_far.append(
            remote(grad_sum.at[(chip + j) % chips], grad_far.at[j - 1], far_sem, (j - 1,), peer(j))
        )
        send_far[j - 1].start()

    lax.fori_loop(1, experts - 1, own_step, 0)

    send_mix.wait_recv()
    mix_got[...] = jnp.concatenate([mix_far[...], rest], axis=0).T

    def far_rows(c):
        part = pl.ds(c * chunk_rows, chunk_rows)
        send_tok[c].wait_recv()

        def far_step(e, carry):
            pick(mix_got, col_far, e)
            gate_up(far_tok, part, col_far, hid_far, e)
            return carry

        lax.fori_loop(0, experts, far_step, 0)

    def down(hid_part, t):
        return jnp.dot(
            hid_part,
            down_s[:, t * tile_cols : (t + 1) * tile_cols],
            preferred_element_type=jnp.float32,
        )

    send_back = []

    def far_down(c):
        part = pl.ds(c * chunk_rows, chunk_rows)
        for t in range(tiles):
            back_send[c, t] = down(hid_far[part, :], t).astype(jnp.bfloat16)
            copy = remote(back_send.at[c, t], back.at[c, t], back_sem, (c, t), partner)
            copy.start()
            send_back.append(copy)

    for copy in weights[2 * experts - 2 : 2 * experts]:
        copy.wait()
    far_rows(0)
    for copy in weights[2 * experts :]:
        copy.wait()
    far_down(0)
    for c in range(1, chunks - 1):
        far_rows(c)
        far_down(c)
    far_rows(chunks - 1)

    for copy in send_far:
        copy.wait_recv()
    total = grad_sum[chip]
    for j in range(1, chips):
        total = total + grad_far[j - 1]
    mean = total / reps
    squares = mean * mean
    square = squares[0:8]
    for i in range(8, frag_rows, 8):
        square = square + squares[i : i + 8]
    sq_own[...] = square
    mean_s[...] = mean
    upd[rep, 1] = mean.astype(jnp.bfloat16)
    send_upd = []
    for j in range(1, chips):
        send_upd.append(remote(upd.at[rep, 1], upd.at[rep, 1], upd_sem, (j - 1,), peer(j)))
        send_upd[j - 1].start()
    forward = [remote(upd.at[rep], upd.at[rep], fwd_sem, (0,), sibling)]
    forward[0].start()
    send_sq = []
    for j in range(1, chips):
        send_sq.append(remote(sq_own, sq_far.at[j - 1], sq_sem, (j - 1,), peer(j)))
        send_sq[j - 1].start()
    far_down(chunks - 1)

    own_rows(experts - 1)
    for copy in send_sq:
        copy.wait_recv()
    square = sq_own[...]
    for j in range(1, chips):
        square = square + sq_far[j - 1]
    sq_chip[...] = square
    to_sib = remote(sq_chip, sq_sib, one_sem, (0,), sibling)
    to_sib.start()

    def own_down(t):
        sum_own[:, t * tile_cols : (t + 1) * tile_cols] = down(hid_own[...], t)

    own_down(0)
    to_sib.wait_recv()
    sq_half[...] = sq_chip[...] + sq_sib[...]
    to_other = remote(sq_half, sq_other, one_sem, (1,), partner)
    to_other.start()
    for t in range(1, tiles):
        own_down(t)

    for j in range(1, chips):
        send_mom[j - 1].wait_recv()
        send_upd[j - 1].wait_recv()
        came = ((chip - j + chips) % chips) * 2 + core
        forward.append(remote(upd.at[came], upd.at[came], fwd_sem, (j,), sibling))
        forward[j].start()

    stores = []

    def combine(c):
        part = pl.ds(c * chunk_rows, chunk_rows)
        for t in range(tiles):
            send_back[c * tiles + t].wait_recv()
            cols = pl.ds(t * tile_cols, tile_cols)
            out_s[part, cols] = (sum_own[part, cols] + back[c, t].astype(jnp.float32)).astype(
                jnp.bfloat16
            )
        stores.append(pltpu.make_async_copy(out_s.at[part], moe_out.at[part], out_sem.at[2 + c]))
        stores[c].start()

    for c in range(chunks - 1):
        combine(c)

    to_other.wait_recv()
    entries = float(frag_rows * 2 * width)
    square_sum = jnp.sum(sq_half[...] + sq_other[...])
    clip_factor = jnp.minimum(1.0, lax.rsqrt(square_sum / entries + clip_epsilon))
    mom_out[...] = outer_momentum * mom_s[...] + clip_factor * mean_s[...]
    store_mom = pltpu.make_async_copy(mom_out, momentum_next, out_sem.at[0])
    store_mom.start()
    load_loc.wait()
    load_glob.wait()

    def merge(index):
        cols = columns(index)
        clipped = clip_factor * upd[index, 1].astype(jnp.float32)
        fresh = outer_momentum * upd[index, 0].astype(jnp.float32) + clipped
        later = glob_s[:, cols] - outer_rate * (outer_momentum * fresh + clipped)
        merged = merge_weight * loc_s[:, cols].astype(jnp.float32) + (1.0 - merge_weight) * later
        loc_out[:, cols] = merged.astype(jnp.bfloat16)

    for j in range(chips):
        merge(((chip - j + chips) % chips) * 2 + core)
    for j in range(chips):
        forward[j].wait_recv()
        merge(((chip - j + chips) % chips) * 2 + 1 - core)
    store_loc = pltpu.make_async_copy(loc_out, local_next.at[0], out_sem.at[1])
    store_loc.start()

    combine(chunks - 1)

    for copy in [send_mix, to_sib, to_other] + send_tok + send_sib + send_far + send_sq + send_back:
        copy.wait_send()
    for copy in send_mom + send_upd + forward:
        copy.wait_send()
    for copy in stores + [store_mom, store_loc]:
        copy.wait()


def closing(moe_in, momentum_in, local_in, moe_out, momentum_next, local_next, sems):
    copies = []
    for source, target in ((moe_in, moe_out), (local_in.at[0], local_next.at[0])):
        half = source.shape[0] // 2
        for k in range(2):
            part = pl.ds(k * half, half)
            sem = sems.at[len(copies)]
            copies.append(pltpu.make_async_copy(source.at[part], target.at[part], sem))
    copies.append(pltpu.make_async_copy(momentum_in, momentum_next, sems.at[4]))
    for copy in copies:
        copy.start()
    for copy in copies:
        copy.wait()


def fused(
    reps,
    tokens,
    routes,
    route_weight,
    w_gate,
    w_up,
    w_down,
    pseudo_grad,
    global_params,
    momentum,
    local_params,
):
    rows, width = tokens.shape
    experts, _, hidden = w_gate.shape
    frag_rows = momentum.shape[0]
    chips = reps // 2
    chunks, tiles = 2, 4
    f32, bf16 = jnp.float32, jnp.bfloat16
    anywhere = pl.BlockSpec(memory_space=pl.ANY)
    in_vmem = pl.BlockSpec(memory_space=pltpu.VMEM)
    dma = pltpu.SemaphoreType.DMA
    block = (frag_rows, LANES)
    returned = (chunks, tiles, rows // chunks, width // tiles)
    out_shape = (
        jax.ShapeDtypeStruct(tokens.shape, tokens.dtype),
        jax.ShapeDtypeStruct(momentum.shape, momentum.dtype),
        jax.ShapeDtypeStruct(local_params.shape, local_params.dtype),
    )
    results = pl.pallas_call(
        functools.partial(kernel, reps),
        out_shape=out_shape,
        in_specs=[anywhere, in_vmem, in_vmem] + [anywhere] * 7,
        out_specs=(anywhere,) * 3,
        scratch_shapes=[
            pltpu.VMEM(w_gate.shape, bf16),
            pltpu.VMEM(w_up.shape, bf16),
            pltpu.VMEM((experts * hidden, width), bf16),
            pltpu.VMEM(tokens.shape, bf16),
            pltpu.VMEM(tokens.shape, bf16),
            pltpu.VMEM((rows, LANES), f32),
            pltpu.VMEM((8, rows), f32),
            pltpu.VMEM((8, rows), f32),
            pltpu.VMEM((rows, LANES), f32),
            pltpu.VMEM((rows, LANES), f32),
            pltpu.VMEM((rows, LANES), f32),
            pltpu.VMEM((rows, experts * hidden), bf16),
            pltpu.VMEM((rows, experts * hidden), bf16),
            pltpu.VMEM((rows, width), f32),
            pltpu.VMEM(returned, bf16),
            pltpu.VMEM(returned, bf16),
            pltpu.VMEM(tokens.shape, bf16),
            pltpu.VMEM((chips,) + block, f32),
            pltpu.VMEM((chips,) + block, f32),
            pltpu.VMEM((chips,) + block, f32),
            pltpu.VMEM((chips - 1,) + block, f32),
            pltpu.VMEM((8, LANES), f32),
            pltpu.VMEM((chips - 1, 8, LANES), f32),
            pltpu.VMEM((8, LANES), f32),
            pltpu.VMEM((8, LANES), f32),
            pltpu.VMEM((8, LANES), f32),
            pltpu.VMEM((8, LANES), f32),
            pltpu.VMEM(block, f32),
            pltpu.VMEM(block, f32),
            pltpu.VMEM((frag_rows, width), f32),
            pltpu.VMEM((frag_rows, width), bf16),
            pltpu.VMEM((reps, 2) + block, bf16),
            pltpu.VMEM(block, f32),
            pltpu.VMEM((frag_rows, width), bf16),
            dma((3, experts)),
            dma((4,)),
            dma((2 + chunks,)),
            dma((chips,)),
            dma((2, chunks)),
            dma((2, 1)),
            dma((2, chunks, tiles)),
            dma((2, chips)),
            dma((2, chips - 1)),
            dma((2, chips - 1)),
            dma((2, 2)),
            dma((2, chips - 1)),
            dma((2, chips - 1)),
            dma((2, chips)),
        ],
        compiler_params=pltpu.CompilerParams(
            collective_id=0, has_side_effects=True, vmem_limit_bytes=56 * 1024 * 1024
        ),
        cost_estimate=pl.CostEstimate(
            flops=12 * rows * experts * hidden * width,
            bytes_accessed=6 * experts * hidden * width,
            transcendentals=0,
        ),
    )(
        tokens,
        routes.T,
        route_weight.T,
        w_gate,
        w_up,
        w_down,
        pseudo_grad,
        global_params,
        momentum,
        local_params,
    )
    return pl.pallas_call(
        closing,
        out_shape=out_shape,
        in_specs=[anywhere] * 3,
        out_specs=(anywhere,) * 3,
        scratch_shapes=[dma((5,))],
        compiler_params=pltpu.CompilerParams(vmem_limit_bytes=60 * 1024 * 1024),
    )(*results)


def solution(mesh):
    in_specs = (
        P(("rep", "shard"), None),
        P(("rep", "shard"), None),
        P(("rep", "shard"), None),
        P("shard", None, None),
        P("shard", None, None),
        P("shard", None, None),
        P("rep", "shard", None),
        P("shard", None),
        P("shard", "rep"),
        P("rep", "shard", None),
    )
    out_specs = (P(("rep", "shard"), None), P("shard", "rep"), P("rep", "shard", None))
    reps, shards = mesh.shape["rep"], mesh.shape["shard"]

    def step(*arrays):
        tokens, w_gate, momentum = arrays[0], arrays[3], arrays[8]
        pairs = shards == 2 and reps % 2 == 0 and reps >= 4
        aligned = momentum.shape[1] == LANES and tokens.shape[0] == LANES
        if pairs and aligned and w_gate.shape[0] * shards == 8:
            return fused(reps, *arrays)
        return local(*arrays)

    return jax.shard_map(step, mesh=mesh, in_specs=in_specs, out_specs=out_specs, check_vma=False)
```

```python
import functools

import jax
import jax.numpy as jnp
from jax import lax
from jax.experimental import pallas as pl
from jax.experimental.pallas import tpu as pltpu
from jax.sharding import PartitionSpec as P

outer_momentum = 0.9
outer_rate = 0.7
merge_weight = 0.5
clip_epsilon = 1e-06


def slot_table(flat_routes, experts, capacity):
    one_hot = (flat_routes[:, None] == jnp.arange(experts, dtype=jnp.int32)[None, :]).astype(
        jnp.int32
    )
    earlier = jnp.cumsum(one_hot, axis=0) - one_hot
    position = jnp.sum(earlier * one_hot, axis=1)
    return flat_routes * capacity + position


def local(
    tokens,
    routes,
    route_weight,
    w_gate,
    w_up,
    w_down,
    pseudo_grad,
    global_params,
    momentum,
    local_params,
):
    tok_rows, feat_width = tokens.shape
    top_count = routes.shape[1]
    local_experts = w_gate.shape[0]
    experts = local_experts * lax.axis_size("shard")
    capacity = tok_rows * 3 // 8
    slot_index = slot_table(routes.reshape(-1), experts, capacity)
    matches = (
        jnp.arange(experts * capacity, dtype=jnp.int32)[:, None] == slot_index[None, :]
    ).astype(jnp.bfloat16)
    placement = jnp.sum(matches.reshape(experts * capacity, tok_rows, top_count), axis=2)
    outgoing = jnp.dot(placement, tokens, preferred_element_type=jnp.float32).astype(jnp.bfloat16)
    outgoing = outgoing.reshape(experts, capacity, feat_width)
    received = lax.all_to_all(outgoing, "shard", split_axis=0, concat_axis=0, tiled=True)
    total_rows = received.shape[0]
    slot_count = received.shape[1]
    grouped = received.reshape(total_rows // local_experts, local_experts, slot_count, feat_width)
    gate = jnp.einsum("spcd,pdf->spcf", grouped, w_gate, preferred_element_type=jnp.float32)
    upward = jnp.einsum("spcd,pdf->spcf", grouped, w_up, preferred_element_type=jnp.float32)
    hidden = (jax.nn.silu(gate) * upward).astype(jnp.bfloat16)
    result = jnp.einsum(
        "spcf,pfd->spcd", hidden, w_down, preferred_element_type=jnp.float32
    ).astype(jnp.bfloat16)
    result = result.reshape(total_rows, slot_count, feat_width)
    returned = lax.all_to_all(result, "shard", split_axis=0, concat_axis=0, tiled=True)
    picked = returned.reshape(experts * capacity, feat_width)[slot_index]
    picked = picked.reshape(tok_rows, top_count, feat_width).astype(jnp.float32)
    moe_out = jnp.sum(route_weight[:, :, None] * picked, axis=1).astype(jnp.bfloat16)
    replicas = lax.axis_size("rep")
    own_delta = pseudo_grad[0]
    frag_rows = own_delta.shape[0]
    entry_count = float(frag_rows * lax.axis_size("shard") * feat_width)
    col_width = momentum.shape[1]
    col_start = lax.axis_index("rep") * col_width
    delta_total = lax.psum(own_delta, "rep")
    mean_delta = delta_total / replicas
    square_sum = lax.psum(jnp.sum(mean_delta * mean_delta), "shard")
    clip_factor = jnp.minimum(1.0, lax.rsqrt(square_sum / entry_count + clip_epsilon))
    clipped = clip_factor * mean_delta
    full_momentum = lax.all_gather(momentum, "rep", axis=1, tiled=True)
    momentum_full = outer_momentum * full_momentum + clipped
    global_next = global_params - outer_rate * (outer_momentum * momentum_full + clipped)
    momentum_next = lax.dynamic_slice_in_dim(momentum_full, col_start, col_width, 1)
    local_next = (
        merge_weight * local_params.astype(jnp.float32) + (1.0 - merge_weight) * global_next[None]
    ).astype(jnp.bfloat16)
    return (moe_out, momentum_next, local_next)


LANES = 128
MESH = pl.DeviceIdType.MESH


def kernel(
    reps,
    tokens,
    routes,
    route_weight,
    w_gate,
    w_up,
    w_down,
    pseudo_grad,
    global_params,
    momentum,
    local_params,
    moe_out,
    momentum_next,
    local_next,
    gate_s,
    up_s,
    down_s,
    tok,
    mix_all,
    mix_send,
    mix_far,
    hid,
    sum_own,
    back_send,
    back,
    out_s,
    grad_own,
    grad_sib,
    grad_sum,
    grad_far,
    sq_own,
    sq_far,
    sq_chip,
    sq_sib,
    sq_half,
    sq_other,
    mean_s,
    mom_s,
    glob_s,
    loc_s,
    upd,
    mom_out,
    loc_out,
    w_sem,
    in_sem,
    out_sem,
    g_sem,
    tok_sem,
    mix_sem,
    back_sem,
    sib_sem,
    far_sem,
    sq_sem,
    one_sem,
    mom_sem,
    upd_sem,
    fwd_sem,
):
    experts = w_gate.shape[0]
    rows, width = tokens.shape
    hidden = w_gate.shape[2]
    chunks, tiles, chunk_rows, tile_cols = back.shape
    frag_rows = momentum.shape[0]
    chips = reps // 2

    rep = lax.axis_index("rep")
    shard = lax.axis_index("shard")
    chip = rep // 2
    core = rep % 2
    partner = (rep, 1 - shard)
    sibling = (chip * 2 + 1 - core, shard)

    def peer(step):
        return (((chip + step) % chips) * 2 + core, shard)

    def columns(index):
        return pl.ds(pl.multiple_of(index * LANES, LANES), LANES)

    weights = []
    for e in range(experts):
        weights.append(pltpu.make_async_copy(w_gate.at[e], gate_s.at[e], w_sem.at[0, e]))
        weights.append(pltpu.make_async_copy(w_up.at[e], up_s.at[e], w_sem.at[1, e]))
    for e in range(experts):
        weights.append(
            pltpu.make_async_copy(w_down.at[e], down_s.at[pl.ds(e * hidden, hidden)], w_sem.at[2, e])
        )
    load_tok = pltpu.make_async_copy(tokens, tok.at[pl.ds(0, rows)], in_sem.at[0])
    load_glob = pltpu.make_async_copy(global_params, glob_s, in_sem.at[1])
    load_mom = pltpu.make_async_copy(momentum, mom_s, in_sem.at[2])
    load_loc = pltpu.make_async_copy(local_params.at[0], loc_s, in_sem.at[3])
    load_grad = [
        pltpu.make_async_copy(
            pseudo_grad.at[0, :, columns(2 * k + core)], grad_own.at[k], g_sem.at[k]
        )
        for k in range(chips)
    ]

    load_mom.start()
    load_tok.start()
    for copy in weights[:2]:
        copy.start()
    for copy in load_grad:
        copy.start()

    ids = lax.broadcasted_iota(jnp.int32, (8, rows), 0)
    mix = jnp.zeros((8, rows), jnp.float32)
    for k in range(routes.shape[0]):
        mix = mix + jnp.where(ids == routes[k : k + 1, :], route_weight[k : k + 1, :], 0.0)
    mix_send[...] = mix
    rest = jnp.zeros((LANES - 8, rows), jnp.float32)
    mix_all[pl.ds(0, rows), :] = jnp.concatenate([mix, rest], axis=0).T

    barrier = pltpu.get_barrier_semaphore()
    for device in [partner, sibling] + [peer(j) for j in range(1, chips)]:
        pl.semaphore_signal(barrier, inc=1, device_id=device, device_id_type=MESH)
    pl.semaphore_wait(barrier, 1 + chips)

    def remote(src, dst, sems, index, device):
        return pltpu.make_async_remote_copy(
            src_ref=src,
            dst_ref=dst,
            send_sem=sems.at[(0,) + index],
            recv_sem=sems.at[(1,) + index],
            device_id=device,
            device_id_type=MESH,
        )

    send_mix = remote(mix_send, mix_far, mix_sem, (0,), partner)
    send_mix.start()
    send_tok = []
    for c in range(chunks):
        part = pl.ds(c * chunk_rows, chunk_rows)
        there = tok.at[pl.ds(rows + c * chunk_rows, chunk_rows)]
        send_tok.append(remote(tokens.at[part], there, tok_sem, (c,), partner))
        send_tok[c].start()
    send_sib = []
    for k in range(chips):
        send_sib.append(
            remote(
                pseudo_grad.at[0, :, columns(2 * k + 1 - core)], grad_sib.at[k], sib_sem, (k,), sibling
            )
        )
        send_sib[k].start()
    load_mom.wait()
    upd[rep, 0] = mom_s[...].astype(jnp.bfloat16)
    send_mom = []
    for j in range(1, chips):
        send_mom.append(remote(upd.at[rep, 0], upd.at[rep, 0], mom_sem, (j - 1,), peer(j)))
        send_mom[j - 1].start()
    for copy in weights[2:]:
        copy.start()
    load_loc.start()
    load_glob.start()

    def gate_up(start, count, e):
        part = pl.ds(start, count)
        lanes = lax.broadcasted_iota(jnp.int32, (count, LANES), 1)
        chosen = jnp.where(lanes == shard * experts + e, mix_all[part, :], 0.0)
        scale = jnp.sum(chosen, axis=1, keepdims=True)
        tok_part = tok[part, :]
        for f in range(0, hidden, 256):
            gate = jnp.dot(tok_part, gate_s[e, :, f : f + 256], preferred_element_type=jnp.float32)
            upward = jnp.dot(tok_part, up_s[e, :, f : f + 256], preferred_element_type=jnp.float32)
            value = gate / (1.0 + jnp.exp(-gate)) * upward * scale
            hid[part, pl.ds(pl.multiple_of(e * hidden + f, LANES), 256)] = value.astype(jnp.bfloat16)

    def weights_in(e):
        pltpu.make_async_copy(w_gate.at[e], gate_s.at[e], w_sem.at[0, e]).wait()
        pltpu.make_async_copy(w_up.at[e], up_s.at[e], w_sem.at[1, e]).wait()

    def steps(start, count, first, last, fresh):
        def one(e, carry):
            if fresh:
                weights_in(e)
            gate_up(start, count, e)
            return carry

        lax.fori_loop(first, last, one, 0)

    early = experts // 2
    load_tok.wait()
    steps(0, rows, 0, 1, True)

    for copy in load_grad:
        copy.wait()
    for copy in send_sib:
        copy.wait_recv()

    def chip_sum(k, carry):
        grad_sum[k] = grad_own[k] + grad_sib[k]
        return carry

    lax.fori_loop(0, chips, chip_sum, 0)
    send_far = []
    for j in range(1, chips):
        send_far.append(
            remote(grad_sum.at[(chip + j) % chips], grad_far.at[j - 1], far_sem, (j - 1,), peer(j))
        )
        send_far[j - 1].start()

    steps(0, rows, 1, early, True)

    send_mix.wait_recv()
    mix_all[pl.ds(rows, rows), :] = jnp.concatenate([mix_far[...], rest], axis=0).T
    send_tok[0].wait_recv()
    steps(rows, chunk_rows, 0, early, False)
    steps(0, rows + chunk_rows, early, experts, True)
    for copy in weights[2 * experts :]:
        copy.wait()

    def down(start, count, t):
        return jnp.dot(
            hid[pl.ds(start, count), :],
            down_s[:, t * tile_cols : (t + 1) * tile_cols],
            preferred_element_type=jnp.float32,
        )

    send_back = []

    def give_back(c, t, value):
        back_send[c, t] = value.astype(jnp.bfloat16)
        copy = remote(back_send.at[c, t], back.at[c, t], back_sem, (c, t), partner)
        copy.start()
        send_back.append(copy)

    for t in range(tiles):
        both = down(0, rows + chunk_rows, t)
        give_back(0, t, both[rows:])
        sum_own[:, t * tile_cols : (t + 1) * tile_cols] = both[:rows]

    for copy in send_far:
        copy.wait_recv()
    total = grad_sum[chip]
    for j in range(1, chips):
        total = total + grad_far[j - 1]
    mean = total / reps
    squares = mean * mean
    square = squares[0:8]
    for i in range(8, frag_rows, 8):
        square = square + squares[i : i + 8]
    sq_own[...] = square
    mean_s[...] = mean
    upd[rep, 1] = mean.astype(jnp.bfloat16)
    send_upd = []
    for j in range(1, chips):
        send_upd.append(remote(upd.at[rep, 1], upd.at[rep, 1], upd_sem, (j - 1,), peer(j)))
        send_upd[j - 1].start()
    forward = [remote(upd.at[rep], upd.at[rep], fwd_sem, (0,), sibling)]
    forward[0].start()
    send_sq = []
    for j in range(1, chips):
        send_sq.append(remote(sq_own, sq_far.at[j - 1], sq_sem, (j - 1,), peer(j)))
        send_sq[j - 1].start()
    send_tok[1].wait_recv()
    steps(rows + chunk_rows, chunk_rows, 0, early, False)
    for copy in send_sq:
        copy.wait_recv()
    square = sq_own[...]
    for j in range(1, chips):
        square = square + sq_far[j - 1]
    sq_chip[...] = square
    to_sib = remote(sq_chip, sq_sib, one_sem, (0,), sibling)
    to_sib.start()
    steps(rows + chunk_rows, chunk_rows, early, experts, False)
    to_sib.wait_recv()
    sq_half[...] = sq_chip[...] + sq_sib[...]
    to_other = remote(sq_half, sq_other, one_sem, (1,), partner)
    to_other.start()
    for t in range(tiles):
        give_back(1, t, down(rows + chunk_rows, chunk_rows, t))

    for j in range(1, chips):
        send_mom[j - 1].wait_recv()
        send_upd[j - 1].wait_recv()
        came = ((chip - j + chips) % chips) * 2 + core
        forward.append(remote(upd.at[came], upd.at[came], fwd_sem, (j,), sibling))
        forward[j].start()

    stores = []

    def combine(c):
        part = pl.ds(c * chunk_rows, chunk_rows)
        for t in range(tiles):
            send_back[c * tiles + t].wait_recv()
            cols = pl.ds(t * tile_cols, tile_cols)
            out_s[part, cols] = (sum_own[part, cols] + back[c, t].astype(jnp.float32)).astype(
                jnp.bfloat16
            )
        stores.append(pltpu.make_async_copy(out_s.at[part], moe_out.at[part], out_sem.at[2 + c]))
        stores[c].start()

    for c in range(chunks - 1):
        combine(c)

    to_other.wait_recv()
    entries = float(frag_rows * 2 * width)
    square_sum = jnp.sum(sq_half[...] + sq_other[...])
    clip_factor = jnp.minimum(1.0, lax.rsqrt(square_sum / entries + clip_epsilon))
    mom_out[...] = outer_momentum * mom_s[...] + clip_factor * mean_s[...]
    store_mom = pltpu.make_async_copy(mom_out, momentum_next, out_sem.at[0])
    store_mom.start()
    load_loc.wait()
    load_glob.wait()

    def merge(index):
        cols = columns(index)
        clipped = clip_factor * upd[index, 1].astype(jnp.float32)
        fresh = outer_momentum * upd[index, 0].astype(jnp.float32) + clipped
        later = glob_s[:, cols] - outer_rate * (outer_momentum * fresh + clipped)
        merged = merge_weight * loc_s[:, cols].astype(jnp.float32) + (1.0 - merge_weight) * later
        loc_out[:, cols] = merged.astype(jnp.bfloat16)

    for j in range(chips):
        merge(((chip - j + chips) % chips) * 2 + core)
    for j in range(chips):
        forward[j].wait_recv()
        merge(((chip - j + chips) % chips) * 2 + 1 - core)
    store_loc = pltpu.make_async_copy(loc_out, local_next.at[0], out_sem.at[1])
    store_loc.start()

    combine(chunks - 1)

    for copy in [send_mix, to_sib, to_other] + send_tok + send_sib + send_far + send_sq + send_back:
        copy.wait_send()
    for copy in send_mom + send_upd + forward:
        copy.wait_send()
    for copy in stores + [store_mom, store_loc]:
        copy.wait()


def closing(moe_in, momentum_in, local_in, moe_out, momentum_next, local_next, moe_s, mom_s, loc_s, sems):
    pieces = [(momentum_in, mom_s, momentum_next)]
    for source, middle, target in ((moe_in, moe_s, moe_out), (local_in.at[0], loc_s, local_next.at[0])):
        half = source.shape[0] // 2
        for k in range(2):
            part = pl.ds(k * half, half)
            pieces.append((source.at[part], middle.at[part], target.at[part]))
    loads, stores = [], []
    for k, (source, middle, target) in enumerate(pieces):
        loads.append(pltpu.make_async_copy(source, middle, sems.at[0, k]))
        stores.append(pltpu.make_async_copy(middle, target, sems.at[1, k]))
        loads[k].start()
    for load, store in zip(loads, stores):
        load.wait()
        store.start()
    for store in stores:
        store.wait()


def fused(
    reps,
    tokens,
    routes,
    route_weight,
    w_gate,
    w_up,
    w_down,
    pseudo_grad,
    global_params,
    momentum,
    local_params,
):
    rows, width = tokens.shape
    experts, _, hidden = w_gate.shape
    frag_rows = momentum.shape[0]
    chips = reps // 2
    chunks, tiles = 2, 4
    f32, bf16 = jnp.float32, jnp.bfloat16
    anywhere = pl.BlockSpec(memory_space=pl.ANY)
    in_vmem = pl.BlockSpec(memory_space=pltpu.VMEM)
    dma = pltpu.SemaphoreType.DMA
    block = (frag_rows, LANES)
    returned = (chunks, tiles, rows // chunks, width // tiles)
    out_shape = (
        jax.ShapeDtypeStruct(tokens.shape, tokens.dtype),
        jax.ShapeDtypeStruct(momentum.shape, momentum.dtype),
        jax.ShapeDtypeStruct(local_params.shape, local_params.dtype),
    )
    results = pl.pallas_call(
        functools.partial(kernel, reps),
        out_shape=out_shape,
        in_specs=[anywhere, in_vmem, in_vmem] + [anywhere] * 7,
        out_specs=(anywhere,) * 3,
        scratch_shapes=[
            pltpu.VMEM(w_gate.shape, bf16),
            pltpu.VMEM(w_up.shape, bf16),
            pltpu.VMEM((experts * hidden, width), bf16),
            pltpu.VMEM((2 * rows, width), bf16),
            pltpu.VMEM((2 * rows, LANES), f32),
            pltpu.VMEM((8, rows), f32),
            pltpu.VMEM((8, rows), f32),
            pltpu.VMEM((2 * rows, experts * hidden), bf16),
            pltpu.VMEM((rows, width), f32),
            pltpu.VMEM(returned, bf16),
            pltpu.VMEM(returned, bf16),
            pltpu.VMEM(tokens.shape, bf16),
            pltpu.VMEM((chips,) + block, f32),
            pltpu.VMEM((chips,) + block, f32),
            pltpu.VMEM((chips,) + block, f32),
            pltpu.VMEM((chips - 1,) + block, f32),
            pltpu.VMEM((8, LANES), f32),
            pltpu.VMEM((chips - 1, 8, LANES), f32),
            pltpu.VMEM((8, LANES), f32),
            pltpu.VMEM((8, LANES), f32),
            pltpu.VMEM((8, LANES), f32),
            pltpu.VMEM((8, LANES), f32),
            pltpu.VMEM(block, f32),
            pltpu.VMEM(block, f32),
            pltpu.VMEM((frag_rows, width), f32),
            pltpu.VMEM((frag_rows, width), bf16),
            pltpu.VMEM((reps, 2) + block, bf16),
            pltpu.VMEM(block, f32),
            pltpu.VMEM((frag_rows, width), bf16),
            dma((3, experts)),
            dma((4,)),
            dma((2 + chunks,)),
            dma((chips,)),
            dma((2, chunks)),
            dma((2, 1)),
            dma((2, chunks, tiles)),
            dma((2, chips)),
            dma((2, chips - 1)),
            dma((2, chips - 1)),
            dma((2, 2)),
            dma((2, chips - 1)),
            dma((2, chips - 1)),
            dma((2, chips)),
        ],
        compiler_params=pltpu.CompilerParams(
            collective_id=0, has_side_effects=True, vmem_limit_bytes=56 * 1024 * 1024
        ),
        cost_estimate=pl.CostEstimate(
            flops=12 * rows * experts * hidden * width,
            bytes_accessed=6 * experts * hidden * width,
            transcendentals=0,
        ),
    )(
        tokens,
        routes.T,
        route_weight.T,
        w_gate,
        w_up,
        w_down,
        pseudo_grad,
        global_params,
        momentum,
        local_params,
    )
    return pl.pallas_call(
        closing,
        out_shape=out_shape,
        in_specs=[anywhere] * 3,
        out_specs=(anywhere,) * 3,
        scratch_shapes=[
            pltpu.VMEM(tokens.shape, bf16),
            pltpu.VMEM(block, f32),
            pltpu.VMEM((frag_rows, width), bf16),
            dma((2, 5)),
        ],
        compiler_params=pltpu.CompilerParams(vmem_limit_bytes=60 * 1024 * 1024),
    )(*results)


def solution(mesh):
    in_specs = (
        P(("rep", "shard"), None),
        P(("rep", "shard"), None),
        P(("rep", "shard"), None),
        P("shard", None, None),
        P("shard", None, None),
        P("shard", None, None),
        P("rep", "shard", None),
        P("shard", None),
        P("shard", "rep"),
        P("rep", "shard", None),
    )
    out_specs = (P(("rep", "shard"), None), P("shard", "rep"), P("rep", "shard", None))
    reps, shards = mesh.shape["rep"], mesh.shape["shard"]

    def step(*arrays):
        tokens, w_gate, momentum = arrays[0], arrays[3], arrays[8]
        pairs = shards == 2 and reps % 2 == 0 and reps >= 4
        aligned = momentum.shape[1] == LANES and tokens.shape[0] == LANES
        if pairs and aligned and w_gate.shape[0] * shards == 8:
            return fused(reps, *arrays)
        return local(*arrays)

    return jax.shard_map(step, mesh=mesh, in_specs=in_specs, out_specs=out_specs, check_vma=False)
```

```python
import functools

import jax
import jax.numpy as jnp
from jax import lax
from jax.experimental import pallas as pl
from jax.experimental.pallas import tpu as pltpu
from jax.sharding import PartitionSpec as P

outer_momentum = 0.9
outer_rate = 0.7
merge_weight = 0.5
clip_epsilon = 1e-06


def slot_table(flat_routes, experts, capacity):
    one_hot = (flat_routes[:, None] == jnp.arange(experts, dtype=jnp.int32)[None, :]).astype(
        jnp.int32
    )
    earlier = jnp.cumsum(one_hot, axis=0) - one_hot
    position = jnp.sum(earlier * one_hot, axis=1)
    return flat_routes * capacity + position


def local(
    tokens,
    routes,
    route_weight,
    w_gate,
    w_up,
    w_down,
    pseudo_grad,
    global_params,
    momentum,
    local_params,
):
    tok_rows, feat_width = tokens.shape
    top_count = routes.shape[1]
    local_experts = w_gate.shape[0]
    experts = local_experts * lax.axis_size("shard")
    capacity = tok_rows * 3 // 8
    slot_index = slot_table(routes.reshape(-1), experts, capacity)
    matches = (
        jnp.arange(experts * capacity, dtype=jnp.int32)[:, None] == slot_index[None, :]
    ).astype(jnp.bfloat16)
    placement = jnp.sum(matches.reshape(experts * capacity, tok_rows, top_count), axis=2)
    outgoing = jnp.dot(placement, tokens, preferred_element_type=jnp.float32).astype(jnp.bfloat16)
    outgoing = outgoing.reshape(experts, capacity, feat_width)
    received = lax.all_to_all(outgoing, "shard", split_axis=0, concat_axis=0, tiled=True)
    total_rows = received.shape[0]
    slot_count = received.shape[1]
    grouped = received.reshape(total_rows // local_experts, local_experts, slot_count, feat_width)
    gate = jnp.einsum("spcd,pdf->spcf", grouped, w_gate, preferred_element_type=jnp.float32)
    upward = jnp.einsum("spcd,pdf->spcf", grouped, w_up, preferred_element_type=jnp.float32)
    hidden = (jax.nn.silu(gate) * upward).astype(jnp.bfloat16)
    result = jnp.einsum(
        "spcf,pfd->spcd", hidden, w_down, preferred_element_type=jnp.float32
    ).astype(jnp.bfloat16)
    result = result.reshape(total_rows, slot_count, feat_width)
    returned = lax.all_to_all(result, "shard", split_axis=0, concat_axis=0, tiled=True)
    picked = returned.reshape(experts * capacity, feat_width)[slot_index]
    picked = picked.reshape(tok_rows, top_count, feat_width).astype(jnp.float32)
    moe_out = jnp.sum(route_weight[:, :, None] * picked, axis=1).astype(jnp.bfloat16)
    replicas = lax.axis_size("rep")
    own_delta = pseudo_grad[0]
    frag_rows = own_delta.shape[0]
    entry_count = float(frag_rows * lax.axis_size("shard") * feat_width)
    col_width = momentum.shape[1]
    col_start = lax.axis_index("rep") * col_width
    delta_total = lax.psum(own_delta, "rep")
    mean_delta = delta_total / replicas
    square_sum = lax.psum(jnp.sum(mean_delta * mean_delta), "shard")
    clip_factor = jnp.minimum(1.0, lax.rsqrt(square_sum / entry_count + clip_epsilon))
    clipped = clip_factor * mean_delta
    full_momentum = lax.all_gather(momentum, "rep", axis=1, tiled=True)
    momentum_full = outer_momentum * full_momentum + clipped
    global_next = global_params - outer_rate * (outer_momentum * momentum_full + clipped)
    momentum_next = lax.dynamic_slice_in_dim(momentum_full, col_start, col_width, 1)
    local_next = (
        merge_weight * local_params.astype(jnp.float32) + (1.0 - merge_weight) * global_next[None]
    ).astype(jnp.bfloat16)
    return (moe_out, momentum_next, local_next)


LANES = 128
STRIP = 256
MESH = pl.DeviceIdType.MESH


def kernel(
    reps,
    tokens,
    routes,
    route_weight,
    w_gate,
    w_up,
    w_down,
    pseudo_grad,
    global_params,
    momentum,
    local_params,
    moe_out,
    momentum_next,
    local_next,
    pair_s,
    down_s,
    tok,
    mix_all,
    mix_send,
    mix_far,
    hid,
    sum_own,
    back_send,
    back,
    out_s,
    grad_own,
    grad_sib,
    grad_sum,
    grad_far,
    sq_own,
    sq_far,
    sq_chip,
    sq_sib,
    sq_half,
    sq_other,
    mean_s,
    mom_s,
    glob_s,
    loc_s,
    upd,
    mom_out,
    loc_out,
    pair_sem,
    w_sem,
    in_sem,
    out_sem,
    g_sem,
    tok_sem,
    mix_sem,
    back_sem,
    sib_sem,
    far_sem,
    sq_sem,
    one_sem,
    mom_sem,
    upd_sem,
    fwd_sem,
):
    experts = w_gate.shape[0]
    rows, width = tokens.shape
    hidden = w_gate.shape[2]
    chunks, tiles, chunk_rows, tile_cols = back.shape
    frag_rows = momentum.shape[0]
    chips = reps // 2

    rep = lax.axis_index("rep")
    shard = lax.axis_index("shard")
    chip = rep // 2
    core = rep % 2
    partner = (rep, 1 - shard)
    sibling = (chip * 2 + 1 - core, shard)

    def peer(step):
        return (((chip + step) % chips) * 2 + core, shard)

    def columns(index):
        return pl.ds(pl.multiple_of(index * LANES, LANES), LANES)

    strips = hidden // STRIP

    def pair_copies(e):
        copies = []
        for f in range(strips):
            for side, source in ((0, w_gate), (1, w_up)):
                copies.append(
                    pltpu.make_async_copy(
                        source.at[e, :, pl.ds(f * STRIP, STRIP)],
                        pair_s.at[e, :, pl.ds((2 * f + side) * STRIP, STRIP)],
                        pair_sem.at[e, 2 * f + side],
                    )
                )
        return copies

    down_copies = [
        pltpu.make_async_copy(w_down.at[e], down_s.at[pl.ds(e * hidden, hidden)], w_sem.at[e])
        for e in range(experts)
    ]
    load_tok = pltpu.make_async_copy(tokens, tok.at[pl.ds(0, rows)], in_sem.at[0])
    load_glob = pltpu.make_async_copy(global_params, glob_s, in_sem.at[1])
    load_mom = pltpu.make_async_copy(momentum, mom_s, in_sem.at[2])
    load_loc = pltpu.make_async_copy(local_params.at[0], loc_s, in_sem.at[3])
    load_grad = [
        pltpu.make_async_copy(
            pseudo_grad.at[0, :, columns(2 * k + core)], grad_own.at[k], g_sem.at[k]
        )
        for k in range(chips)
    ]

    load_mom.start()
    load_tok.start()
    for copy in pair_copies(0):
        copy.start()
    for copy in load_grad:
        copy.start()

    ids = lax.broadcasted_iota(jnp.int32, (8, rows), 0)
    mix = jnp.zeros((8, rows), jnp.float32)
    for k in range(routes.shape[0]):
        mix = mix + jnp.where(ids == routes[k : k + 1, :], route_weight[k : k + 1, :], 0.0)
    mix_send[...] = mix
    rest = jnp.zeros((LANES - 8, rows), jnp.float32)
    mix_all[pl.ds(0, rows), :] = jnp.concatenate([mix, rest], axis=0).T

    barrier = pltpu.get_barrier_semaphore()
    for device in [partner, sibling] + [peer(j) for j in range(1, chips)]:
        pl.semaphore_signal(barrier, inc=1, device_id=device, device_id_type=MESH)
    pl.semaphore_wait(barrier, 1 + chips)

    def remote(src, dst, sems, index, device):
        return pltpu.make_async_remote_copy(
            src_ref=src,
            dst_ref=dst,
            send_sem=sems.at[(0,) + index],
            recv_sem=sems.at[(1,) + index],
            device_id=device,
            device_id_type=MESH,
        )

    send_mix = remote(mix_send, mix_far, mix_sem, (0,), partner)
    send_mix.start()
    send_tok = []
    for c in range(chunks):
        part = pl.ds(c * chunk_rows, chunk_rows)
        there = tok.at[pl.ds(rows + c * chunk_rows, chunk_rows)]
        send_tok.append(remote(tokens.at[part], there, tok_sem, (c,), partner))
        send_tok[c].start()
    send_sib = []
    for k in range(chips):
        send_sib.append(
            remote(
                pseudo_grad.at[0, :, columns(2 * k + 1 - core)], grad_sib.at[k], sib_sem, (k,), sibling
            )
        )
        send_sib[k].start()
    load_mom.wait()
    upd[rep, 0] = mom_s[...].astype(jnp.bfloat16)
    send_mom = []
    for j in range(1, chips):
        send_mom.append(remote(upd.at[rep, 0], upd.at[rep, 0], mom_sem, (j - 1,), peer(j)))
        send_mom[j - 1].start()
    for e in range(1, experts):
        for copy in pair_copies(e):
            copy.start()
    for copy in down_copies:
        copy.start()
    load_loc.start()
    load_glob.start()

    def gate_up(start, count, e):
        part = pl.ds(start, count)
        lanes = lax.broadcasted_iota(jnp.int32, (count, LANES), 1)
        chosen = jnp.where(lanes == shard * experts + e, mix_all[part, :], 0.0)
        scale = jnp.sum(chosen, axis=1, keepdims=True)
        tok_part = tok[part, :]
        for f in range(strips):
            both = pair_s[e, :, 2 * f * STRIP : 2 * (f + 1) * STRIP]
            pair = jnp.dot(tok_part, both, preferred_element_type=jnp.float32)
            gate, upward = pair[:, :STRIP], pair[:, STRIP:]
            value = gate / (1.0 + jnp.exp(-gate)) * upward * scale
            place = pl.ds(pl.multiple_of(e * hidden + f * STRIP, STRIP), STRIP)
            hid[part, place] = value.astype(jnp.bfloat16)

    def weights_in(e):
        for copy in pair_copies(e):
            copy.wait()

    def steps(start, count, first, last, fresh):
        def one(e, carry):
            if fresh:
                weights_in(e)
            gate_up(start, count, e)
            return carry

        lax.fori_loop(first, last, one, 0)

    early = experts // 2
    load_tok.wait()
    steps(0, rows, 0, 1, True)

    for copy in load_grad:
        copy.wait()
    for copy in send_sib:
        copy.wait_recv()

    def chip_sum(k, carry):
        grad_sum[k] = grad_own[k] + grad_sib[k]
        return carry

    lax.fori_loop(0, chips, chip_sum, 0)
    send_far = []
    for j in range(1, chips):
        send_far.append(
            remote(grad_sum.at[(chip + j) % chips], grad_far.at[j - 1], far_sem, (j - 1,), peer(j))
        )
        send_far[j - 1].start()

    steps(0, rows, 1, early, True)

    send_mix.wait_recv()
    mix_all[pl.ds(rows, rows), :] = jnp.concatenate([mix_far[...], rest], axis=0).T
    send_tok[0].wait_recv()
    steps(rows, chunk_rows, 0, early, False)
    steps(0, rows + chunk_rows, early, experts, True)
    for copy in down_copies:
        copy.wait()

    def down(start, count, t):
        return jnp.dot(
            hid[pl.ds(start, count), :],
            down_s[:, t * tile_cols : (t + 1) * tile_cols],
            preferred_element_type=jnp.float32,
        )

    send_back = []

    def give_back(c, t, value):
        back_send[c, t] = value.astype(jnp.bfloat16)
        copy = remote(back_send.at[c, t], back.at[c, t], back_sem, (c, t), partner)
        copy.start()
        send_back.append(copy)

    for t in range(tiles):
        both = down(0, rows + chunk_rows, t)
        give_back(0, t, both[rows:])
        sum_own[:, t * tile_cols : (t + 1) * tile_cols] = both[:rows]

    for copy in send_far:
        copy.wait_recv()
    total = grad_sum[chip]
    for j in range(1, chips):
        total = total + grad_far[j - 1]
    mean = total / reps
    squares = mean * mean
    square = squares[0:8]
    for i in range(8, frag_rows, 8):
        square = square + squares[i : i + 8]
    sq_own[...] = square
    mean_s[...] = mean
    upd[rep, 1] = mean.astype(jnp.bfloat16)
    send_upd = []
    for j in range(1, chips):
        send_upd.append(remote(upd.at[rep, 1], upd.at[rep, 1], upd_sem, (j - 1,), peer(j)))
        send_upd[j - 1].start()
    forward = [remote(upd.at[rep], upd.at[rep], fwd_sem, (0,), sibling)]
    forward[0].start()
    send_sq = []
    for j in range(1, chips):
        send_sq.append(remote(sq_own, sq_far.at[j - 1], sq_sem, (j - 1,), peer(j)))
        send_sq[j - 1].start()
    send_tok[1].wait_recv()
    steps(rows + chunk_rows, chunk_rows, 0, early, False)
    for copy in send_sq:
        copy.wait_recv()
    square = sq_own[...]
    for j in range(1, chips):
        square = square + sq_far[j - 1]
    sq_chip[...] = square
    to_sib = remote(sq_chip, sq_sib, one_sem, (0,), sibling)
    to_sib.start()
    steps(rows + chunk_rows, chunk_rows, early, experts, False)
    to_sib.wait_recv()
    sq_half[...] = sq_chip[...] + sq_sib[...]
    to_other = remote(sq_half, sq_other, one_sem, (1,), partner)
    to_other.start()
    for t in range(tiles):
        give_back(1, t, down(rows + chunk_rows, chunk_rows, t))

    for j in range(1, chips):
        send_mom[j - 1].wait_recv()
        send_upd[j - 1].wait_recv()
        came = ((chip - j + chips) % chips) * 2 + core
        forward.append(remote(upd.at[came], upd.at[came], fwd_sem, (j,), sibling))
        forward[j].start()

    stores = []

    def combine(c):
        part = pl.ds(c * chunk_rows, chunk_rows)
        for t in range(tiles):
            send_back[c * tiles + t].wait_recv()
            cols = pl.ds(t * tile_cols, tile_cols)
            out_s[part, cols] = (sum_own[part, cols] + back[c, t].astype(jnp.float32)).astype(
                jnp.bfloat16
            )
        stores.append(pltpu.make_async_copy(out_s.at[part], moe_out.at[part], out_sem.at[2 + c]))
        stores[c].start()

    for c in range(chunks - 1):
        combine(c)

    to_other.wait_recv()
    entries = float(frag_rows * 2 * width)
    square_sum = jnp.sum(sq_half[...] + sq_other[...])
    clip_factor = jnp.minimum(1.0, lax.rsqrt(square_sum / entries + clip_epsilon))
    mom_out[...] = outer_momentum * mom_s[...] + clip_factor * mean_s[...]
    store_mom = pltpu.make_async_copy(mom_out, momentum_next, out_sem.at[0])
    store_mom.start()
    load_loc.wait()
    load_glob.wait()

    def merge(index):
        cols = columns(index)
        clipped = clip_factor * upd[index, 1].astype(jnp.float32)
        fresh = outer_momentum * upd[index, 0].astype(jnp.float32) + clipped
        later = glob_s[:, cols] - outer_rate * (outer_momentum * fresh + clipped)
        merged = merge_weight * loc_s[:, cols].astype(jnp.float32) + (1.0 - merge_weight) * later
        loc_out[:, cols] = merged.astype(jnp.bfloat16)

    for j in range(chips):
        merge(((chip - j + chips) % chips) * 2 + core)
    for j in range(chips):
        forward[j].wait_recv()
        merge(((chip - j + chips) % chips) * 2 + 1 - core)
    store_loc = pltpu.make_async_copy(loc_out, local_next.at[0], out_sem.at[1])
    store_loc.start()

    combine(chunks - 1)

    for copy in [send_mix, to_sib, to_other] + send_tok + send_sib + send_far + send_sq + send_back:
        copy.wait_send()
    for copy in send_mom + send_upd + forward:
        copy.wait_send()
    for copy in stores + [store_mom, store_loc]:
        copy.wait()


def closing(moe_in, momentum_in, local_in, moe_out, momentum_next, local_next, moe_s, mom_s, loc_s, sems):
    pieces = [(momentum_in, mom_s, momentum_next)]
    for source, middle, target in ((moe_in, moe_s, moe_out), (local_in.at[0], loc_s, local_next.at[0])):
        half = source.shape[0] // 2
        for k in range(2):
            part = pl.ds(k * half, half)
            pieces.append((source.at[part], middle.at[part], target.at[part]))
    loads, stores = [], []
    for k, (source, middle, target) in enumerate(pieces):
        loads.append(pltpu.make_async_copy(source, middle, sems.at[0, k]))
        stores.append(pltpu.make_async_copy(middle, target, sems.at[1, k]))
        loads[k].start()
    for load, store in zip(loads, stores):
        load.wait()
        store.start()
    for store in stores:
        store.wait()


def fused(
    reps,
    tokens,
    routes,
    route_weight,
    w_gate,
    w_up,
    w_down,
    pseudo_grad,
    global_params,
    momentum,
    local_params,
):
    rows, width = tokens.shape
    experts, _, hidden = w_gate.shape
    frag_rows = momentum.shape[0]
    chips = reps // 2
    chunks, tiles = 2, 4
    f32, bf16 = jnp.float32, jnp.bfloat16
    anywhere = pl.BlockSpec(memory_space=pl.ANY)
    in_vmem = pl.BlockSpec(memory_space=pltpu.VMEM)
    dma = pltpu.SemaphoreType.DMA
    block = (frag_rows, LANES)
    returned = (chunks, tiles, rows // chunks, width // tiles)
    out_shape = (
        jax.ShapeDtypeStruct(tokens.shape, tokens.dtype),
        jax.ShapeDtypeStruct(momentum.shape, momentum.dtype),
        jax.ShapeDtypeStruct(local_params.shape, local_params.dtype),
    )
    results = pl.pallas_call(
        functools.partial(kernel, reps),
        out_shape=out_shape,
        in_specs=[anywhere, in_vmem, in_vmem] + [anywhere] * 7,
        out_specs=(anywhere,) * 3,
        scratch_shapes=[
            pltpu.VMEM((experts, width, 2 * hidden), bf16),
            pltpu.VMEM((experts * hidden, width), bf16),
            pltpu.VMEM((2 * rows, width), bf16),
            pltpu.VMEM((2 * rows, LANES), f32),
            pltpu.VMEM((8, rows), f32),
            pltpu.VMEM((8, rows), f32),
            pltpu.VMEM((2 * rows, experts * hidden), bf16),
            pltpu.VMEM((rows, width), f32),
            pltpu.VMEM(returned, bf16),
            pltpu.VMEM(returned, bf16),
            pltpu.VMEM(tokens.shape, bf16),
            pltpu.VMEM((chips,) + block, f32),
            pltpu.VMEM((chips,) + block, f32),
            pltpu.VMEM((chips,) + block, f32),
            pltpu.VMEM((chips - 1,) + block, f32),
            pltpu.VMEM((8, LANES), f32),
            pltpu.VMEM((chips - 1, 8, LANES), f32),
            pltpu.VMEM((8, LANES), f32),
            pltpu.VMEM((8, LANES), f32),
            pltpu.VMEM((8, LANES), f32),
            pltpu.VMEM((8, LANES), f32),
            pltpu.VMEM(block, f32),
            pltpu.VMEM(block, f32),
            pltpu.VMEM((frag_rows, width), f32),
            pltpu.VMEM((frag_rows, width), bf16),
            pltpu.VMEM((reps, 2) + block, bf16),
            pltpu.VMEM(block, f32),
            pltpu.VMEM((frag_rows, width), bf16),
            dma((experts, 2 * hidden // STRIP)),
            dma((experts,)),
            dma((4,)),
            dma((2 + chunks,)),
            dma((chips,)),
            dma((2, chunks)),
            dma((2, 1)),
            dma((2, chunks, tiles)),
            dma((2, chips)),
            dma((2, chips - 1)),
            dma((2, chips - 1)),
            dma((2, 2)),
            dma((2, chips - 1)),
            dma((2, chips - 1)),
            dma((2, chips)),
        ],
        compiler_params=pltpu.CompilerParams(
            collective_id=0, has_side_effects=True, vmem_limit_bytes=56 * 1024 * 1024
        ),
        cost_estimate=pl.CostEstimate(
            flops=12 * rows * experts * hidden * width,
            bytes_accessed=6 * experts * hidden * width,
            transcendentals=0,
        ),
    )(
        tokens,
        routes.T,
        route_weight.T,
        w_gate,
        w_up,
        w_down,
        pseudo_grad,
        global_params,
        momentum,
        local_params,
    )
    return pl.pallas_call(
        closing,
        out_shape=out_shape,
        in_specs=[anywhere] * 3,
        out_specs=(anywhere,) * 3,
        scratch_shapes=[
            pltpu.VMEM(tokens.shape, bf16),
            pltpu.VMEM(block, f32),
            pltpu.VMEM((frag_rows, width), bf16),
            dma((2, 5)),
        ],
        compiler_params=pltpu.CompilerParams(vmem_limit_bytes=60 * 1024 * 1024),
    )(*results)


def solution(mesh):
    in_specs = (
        P(("rep", "shard"), None),
        P(("rep", "shard"), None),
        P(("rep", "shard"), None),
        P("shard", None, None),
        P("shard", None, None),
        P("shard", None, None),
        P("rep", "shard", None),
        P("shard", None),
        P("shard", "rep"),
        P("rep", "shard", None),
    )
    out_specs = (P(("rep", "shard"), None), P("shard", "rep"), P("rep", "shard", None))
    reps, shards = mesh.shape["rep"], mesh.shape["shard"]

    def step(*arrays):
        tokens, w_gate, momentum = arrays[0], arrays[3], arrays[8]
        pairs = shards == 2 and reps % 2 == 0 and reps >= 4
        aligned = momentum.shape[1] == LANES and tokens.shape[0] == LANES
        if pairs and aligned and w_gate.shape[0] * shards == 8:
            return fused(reps, *arrays)
        return local(*arrays)

    return jax.shard_map(step, mesh=mesh, in_specs=in_specs, out_specs=out_specs, check_vma=False)
```

```python
import functools

import jax
import jax.numpy as jnp
from jax import lax
from jax.experimental import pallas as pl
from jax.experimental.pallas import tpu as pltpu
from jax.sharding import PartitionSpec as P

outer_momentum = 0.9
outer_rate = 0.7
merge_weight = 0.5
clip_epsilon = 1e-06


def slot_table(flat_routes, experts, capacity):
    one_hot = (flat_routes[:, None] == jnp.arange(experts, dtype=jnp.int32)[None, :]).astype(
        jnp.int32
    )
    earlier = jnp.cumsum(one_hot, axis=0) - one_hot
    position = jnp.sum(earlier * one_hot, axis=1)
    return flat_routes * capacity + position


def local(
    tokens,
    routes,
    route_weight,
    w_gate,
    w_up,
    w_down,
    pseudo_grad,
    global_params,
    momentum,
    local_params,
):
    tok_rows, feat_width = tokens.shape
    top_count = routes.shape[1]
    local_experts = w_gate.shape[0]
    experts = local_experts * lax.axis_size("shard")
    capacity = tok_rows * 3 // 8
    slot_index = slot_table(routes.reshape(-1), experts, capacity)
    matches = (
        jnp.arange(experts * capacity, dtype=jnp.int32)[:, None] == slot_index[None, :]
    ).astype(jnp.bfloat16)
    placement = jnp.sum(matches.reshape(experts * capacity, tok_rows, top_count), axis=2)
    outgoing = jnp.dot(placement, tokens, preferred_element_type=jnp.float32).astype(jnp.bfloat16)
    outgoing = outgoing.reshape(experts, capacity, feat_width)
    received = lax.all_to_all(outgoing, "shard", split_axis=0, concat_axis=0, tiled=True)
    total_rows = received.shape[0]
    slot_count = received.shape[1]
    grouped = received.reshape(total_rows // local_experts, local_experts, slot_count, feat_width)
    gate = jnp.einsum("spcd,pdf->spcf", grouped, w_gate, preferred_element_type=jnp.float32)
    upward = jnp.einsum("spcd,pdf->spcf", grouped, w_up, preferred_element_type=jnp.float32)
    hidden = (jax.nn.silu(gate) * upward).astype(jnp.bfloat16)
    result = jnp.einsum(
        "spcf,pfd->spcd", hidden, w_down, preferred_element_type=jnp.float32
    ).astype(jnp.bfloat16)
    result = result.reshape(total_rows, slot_count, feat_width)
    returned = lax.all_to_all(result, "shard", split_axis=0, concat_axis=0, tiled=True)
    picked = returned.reshape(experts * capacity, feat_width)[slot_index]
    picked = picked.reshape(tok_rows, top_count, feat_width).astype(jnp.float32)
    moe_out = jnp.sum(route_weight[:, :, None] * picked, axis=1).astype(jnp.bfloat16)
    replicas = lax.axis_size("rep")
    own_delta = pseudo_grad[0]
    frag_rows = own_delta.shape[0]
    entry_count = float(frag_rows * lax.axis_size("shard") * feat_width)
    col_width = momentum.shape[1]
    col_start = lax.axis_index("rep") * col_width
    delta_total = lax.psum(own_delta, "rep")
    mean_delta = delta_total / replicas
    square_sum = lax.psum(jnp.sum(mean_delta * mean_delta), "shard")
    clip_factor = jnp.minimum(1.0, lax.rsqrt(square_sum / entry_count + clip_epsilon))
    clipped = clip_factor * mean_delta
    full_momentum = lax.all_gather(momentum, "rep", axis=1, tiled=True)
    momentum_full = outer_momentum * full_momentum + clipped
    global_next = global_params - outer_rate * (outer_momentum * momentum_full + clipped)
    momentum_next = lax.dynamic_slice_in_dim(momentum_full, col_start, col_width, 1)
    local_next = (
        merge_weight * local_params.astype(jnp.float32) + (1.0 - merge_weight) * global_next[None]
    ).astype(jnp.bfloat16)
    return (moe_out, momentum_next, local_next)


LANES = 128
STRIP = 256
MESH = pl.DeviceIdType.MESH


def kernel(
    reps,
    tokens,
    routes,
    route_weight,
    w_gate,
    w_up,
    w_down,
    pseudo_grad,
    global_params,
    momentum,
    local_params,
    moe_out,
    momentum_next,
    local_next,
    pair_s,
    down_s,
    tok,
    mix_all,
    mix_send,
    mix_far,
    hid,
    sum_own,
    back_send,
    back,
    out_s,
    grad_own,
    grad_sib,
    grad_sum,
    grad_half,
    grad_far,
    sq_own,
    sq_far,
    sq_chip,
    sq_sib,
    sq_half,
    sq_other,
    mean_s,
    mom_s,
    glob_s,
    loc_s,
    upd,
    mom_out,
    loc_out,
    pair_sem,
    w_sem,
    in_sem,
    out_sem,
    g_sem,
    tok_sem,
    mix_sem,
    back_sem,
    sib_sem,
    far_sem,
    sq_sem,
    one_sem,
    mom_sem,
    upd_sem,
    side_sem,
    fwd_sem,
):
    experts = w_gate.shape[0]
    rows, width = tokens.shape
    hidden = w_gate.shape[2]
    chunks, tiles, chunk_rows, tile_cols = back.shape
    frag_rows = momentum.shape[0]
    chips = reps // 2

    rep = lax.axis_index("rep")
    shard = lax.axis_index("shard")
    chip = rep // 2
    core = rep % 2
    partner = (rep, 1 - shard)
    sibling = (chip * 2 + 1 - core, shard)

    def peer(step):
        return (((chip + step) % chips) * 2 + core, shard)

    def columns(index):
        return pl.ds(pl.multiple_of(index * LANES, LANES), LANES)

    strips = hidden // STRIP

    def pair_copies(e):
        copies = []
        for f in range(strips):
            for side, source in ((0, w_gate), (1, w_up)):
                copies.append(
                    pltpu.make_async_copy(
                        source.at[e, :, pl.ds(f * STRIP, STRIP)],
                        pair_s.at[e, :, pl.ds((2 * f + side) * STRIP, STRIP)],
                        pair_sem.at[e, 2 * f + side],
                    )
                )
        return copies

    down_copies = [
        pltpu.make_async_copy(w_down.at[e], down_s.at[pl.ds(e * hidden, hidden)], w_sem.at[e])
        for e in range(experts)
    ]
    load_tok = pltpu.make_async_copy(tokens, tok.at[pl.ds(0, rows)], in_sem.at[0])
    load_glob = pltpu.make_async_copy(global_params, glob_s, in_sem.at[1])
    load_mom = pltpu.make_async_copy(momentum, mom_s, in_sem.at[2])
    load_loc = pltpu.make_async_copy(local_params.at[0], loc_s, in_sem.at[3])
    load_grad = [
        pltpu.make_async_copy(
            pseudo_grad.at[0, :, columns(2 * k + core)], grad_own.at[k], g_sem.at[k]
        )
        for k in range(chips)
    ]

    load_mom.start()
    load_tok.start()
    for copy in pair_copies(0):
        copy.start()
    for copy in load_grad:
        copy.start()

    ids = lax.broadcasted_iota(jnp.int32, (8, rows), 0)
    mix = jnp.zeros((8, rows), jnp.float32)
    for k in range(routes.shape[0]):
        mix = mix + jnp.where(ids == routes[k : k + 1, :], route_weight[k : k + 1, :], 0.0)
    mix_send[...] = mix
    rest = jnp.zeros((LANES - 8, rows), jnp.float32)
    mix_all[pl.ds(0, rows), :] = jnp.concatenate([mix, rest], axis=0).T

    barrier = pltpu.get_barrier_semaphore()
    for device in [partner, sibling] + [peer(j) for j in range(1, chips)]:
        pl.semaphore_signal(barrier, inc=1, device_id=device, device_id_type=MESH)
    pl.semaphore_wait(barrier, 1 + chips)

    def remote(src, dst, sems, index, device):
        return pltpu.make_async_remote_copy(
            src_ref=src,
            dst_ref=dst,
            send_sem=sems.at[(0,) + index],
            recv_sem=sems.at[(1,) + index],
            device_id=device,
            device_id_type=MESH,
        )

    send_mix = remote(mix_send, mix_far, mix_sem, (0,), partner)
    send_mix.start()
    send_tok = []
    for c in range(chunks):
        part = pl.ds(c * chunk_rows, chunk_rows)
        there = tok.at[pl.ds(rows + c * chunk_rows, chunk_rows)]
        send_tok.append(remote(tokens.at[part], there, tok_sem, (c,), partner))
        send_tok[c].start()
    send_sib = []
    for k in range(chips):
        send_sib.append(
            remote(
                pseudo_grad.at[0, :, columns(2 * k + 1 - core)], grad_sib.at[k], sib_sem, (k,), sibling
            )
        )
        send_sib[k].start()
    load_mom.wait()
    upd[rep, 0] = mom_s[...].astype(jnp.bfloat16)
    send_mom = []
    along = range(2, chips, 2)
    for k, j in enumerate(along):
        send_mom.append(remote(upd.at[rep, 0], upd.at[rep, 0], mom_sem, (k,), peer(j)))
        send_mom[k].start()
    for e in range(1, experts):
        for copy in pair_copies(e):
            copy.start()
    for copy in down_copies:
        copy.start()
    load_loc.start()
    load_glob.start()

    def gate_up(start, count, e):
        part = pl.ds(start, count)
        lanes = lax.broadcasted_iota(jnp.int32, (count, LANES), 1)
        chosen = jnp.where(lanes == shard * experts + e, mix_all[part, :], 0.0)
        scale = jnp.sum(chosen, axis=1, keepdims=True)
        tok_part = tok[part, :]
        for f in range(strips):
            both = pair_s[e, :, 2 * f * STRIP : 2 * (f + 1) * STRIP]
            pair = jnp.dot(tok_part, both, preferred_element_type=jnp.float32)
            gate, upward = pair[:, :STRIP], pair[:, STRIP:]
            value = gate / (1.0 + jnp.exp(-gate)) * upward * scale
            place = pl.ds(pl.multiple_of(e * hidden + f * STRIP, STRIP), STRIP)
            hid[part, place] = value.astype(jnp.bfloat16)

    def weights_in(e):
        for copy in pair_copies(e):
            copy.wait()

    def steps(start, count, first, last, fresh):
        def one(e, carry):
            if fresh:
                weights_in(e)
            gate_up(start, count, e)
            return carry

        lax.fori_loop(first, last, one, 0)

    early = experts // 2
    load_tok.wait()
    steps(0, rows, 0, 1, True)

    for copy in load_grad:
        copy.wait()
    for copy in send_sib:
        copy.wait_recv()

    def chip_sum(k, carry):
        both_cores = grad_own[k] + grad_sib[k]
        grad_sum[k] = both_cores
        grad_half[k] = both_cores.astype(jnp.bfloat16)
        return carry

    lax.fori_loop(0, chips, chip_sum, 0)
    send_far = []
    for j in range(1, chips):
        send_far.append(
            remote(grad_half.at[(chip + j) % chips], grad_far.at[j - 1], far_sem, (j - 1,), peer(j))
        )
        send_far[j - 1].start()

    steps(0, rows, 1, early, True)

    send_mix.wait_recv()
    mix_all[pl.ds(rows, rows), :] = jnp.concatenate([mix_far[...], rest], axis=0).T
    send_tok[0].wait_recv()
    steps(rows, chunk_rows, 0, early, False)
    steps(0, rows + chunk_rows, early, experts, True)
    for copy in down_copies:
        copy.wait()

    def down(start, count, t):
        return jnp.dot(
            hid[pl.ds(start, count), :],
            down_s[:, t * tile_cols : (t + 1) * tile_cols],
            preferred_element_type=jnp.float32,
        )

    send_back = []

    def give_back(c, t, value):
        back_send[c, t] = value.astype(jnp.bfloat16)
        copy = remote(back_send.at[c, t], back.at[c, t], back_sem, (c, t), partner)
        copy.start()
        send_back.append(copy)

    for t in range(tiles):
        both = down(0, rows + chunk_rows, t)
        give_back(0, t, both[rows:])
        sum_own[:, t * tile_cols : (t + 1) * tile_cols] = both[:rows]

    for copy in send_far:
        copy.wait_recv()
    total = grad_sum[chip]
    for j in range(1, chips):
        total = total + grad_far[j - 1].astype(jnp.float32)
    mean = total / reps
    squares = mean * mean
    square = squares[0:8]
    for i in range(8, frag_rows, 8):
        square = square + squares[i : i + 8]
    sq_own[...] = square
    mean_s[...] = mean
    upd[rep, 1] = mean.astype(jnp.bfloat16)
    send_upd = []
    for k, j in enumerate(along):
        send_upd.append(remote(upd.at[rep, 1], upd.at[rep, 1], upd_sem, (k,), peer(j)))
        send_upd[k].start()
    side = chip + 1 - 2 * (chip % 2)
    origins, across, forward = [], [], []

    def pass_on(origin, further):
        came = origin * 2 + core
        if further:
            device = (side * 2 + core, shard)
            across.append(remote(upd.at[came], upd.at[came], side_sem, (len(across),), device))
            across[-1].start()
        forward.append(remote(upd.at[came], upd.at[came], fwd_sem, (len(forward),), sibling))
        forward[-1].start()
        origins.append(origin)

    pass_on(chip, True)
    send_sq = []
    for j in range(1, chips):
        send_sq.append(remote(sq_own, sq_far.at[j - 1], sq_sem, (j - 1,), peer(j)))
        send_sq[j - 1].start()
    send_tok[1].wait_recv()
    steps(rows + chunk_rows, chunk_rows, 0, early, False)
    for copy in send_sq:
        copy.wait_recv()
    square = sq_own[...]
    for j in range(1, chips):
        square = square + sq_far[j - 1]
    sq_chip[...] = square
    to_sib = remote(sq_chip, sq_sib, one_sem, (0,), sibling)
    to_sib.start()
    steps(rows + chunk_rows, chunk_rows, early, experts, False)
    to_sib.wait_recv()
    sq_half[...] = sq_chip[...] + sq_sib[...]
    to_other = remote(sq_half, sq_other, one_sem, (1,), partner)
    to_other.start()
    for t in range(tiles):
        give_back(1, t, down(rows + chunk_rows, chunk_rows, t))
        if t == tiles // 2 - 1:
            for k, j in enumerate(along):
                send_mom[k].wait_recv()
                send_upd[k].wait_recv()
                pass_on((chip - j + chips) % chips, True)
    for k in range(chips // 2):
        across[k].wait_recv()
        pass_on((side - 2 * k + chips) % chips, False)

    stores = []

    def combine(c):
        part = pl.ds(c * chunk_rows, chunk_rows)
        for t in range(tiles):
            send_back[c * tiles + t].wait_recv()
            cols = pl.ds(t * tile_cols, tile_cols)
            out_s[part, cols] = (sum_own[part, cols] + back[c, t].astype(jnp.float32)).astype(
                jnp.bfloat16
            )
        stores.append(pltpu.make_async_copy(out_s.at[part], moe_out.at[part], out_sem.at[2 + c]))
        stores[c].start()

    for c in range(chunks - 1):
        combine(c)

    to_other.wait_recv()
    entries = float(frag_rows * 2 * width)
    square_sum = jnp.sum(sq_half[...] + sq_other[...])
    clip_factor = jnp.minimum(1.0, lax.rsqrt(square_sum / entries + clip_epsilon))
    mom_out[...] = outer_momentum * mom_s[...] + clip_factor * mean_s[...]
    store_mom = pltpu.make_async_copy(mom_out, momentum_next, out_sem.at[0])
    store_mom.start()
    load_loc.wait()
    load_glob.wait()

    def merge(index):
        cols = columns(index)
        clipped = clip_factor * upd[index, 1].astype(jnp.float32)
        fresh = outer_momentum * upd[index, 0].astype(jnp.float32) + clipped
        later = glob_s[:, cols] - outer_rate * (outer_momentum * fresh + clipped)
        merged = merge_weight * loc_s[:, cols].astype(jnp.float32) + (1.0 - merge_weight) * later
        loc_out[:, cols] = merged.astype(jnp.bfloat16)

    for origin in origins:
        merge(origin * 2 + core)
    for copy, origin in zip(forward, origins):
        copy.wait_recv()
        merge(origin * 2 + 1 - core)
    store_loc = pltpu.make_async_copy(loc_out, local_next.at[0], out_sem.at[1])
    store_loc.start()

    combine(chunks - 1)

    for copy in [send_mix, to_sib, to_other] + send_tok + send_sib + send_far + send_sq + send_back:
        copy.wait_send()
    for copy in send_mom + send_upd + across + forward:
        copy.wait_send()
    for copy in stores + [store_mom, store_loc]:
        copy.wait()


def closing(moe_in, momentum_in, local_in, moe_out, momentum_next, local_next, moe_s, mom_s, loc_s, sems):
    pieces = [(momentum_in, mom_s, momentum_next)]
    for source, middle, target in ((moe_in, moe_s, moe_out), (local_in.at[0], loc_s, local_next.at[0])):
        half = source.shape[0] // 2
        for k in range(2):
            part = pl.ds(k * half, half)
            pieces.append((source.at[part], middle.at[part], target.at[part]))
    loads, stores = [], []
    for k, (source, middle, target) in enumerate(pieces):
        loads.append(pltpu.make_async_copy(source, middle, sems.at[0, k]))
        stores.append(pltpu.make_async_copy(middle, target, sems.at[1, k]))
        loads[k].start()
    for load, store in zip(loads, stores):
        load.wait()
        store.start()
    for store in stores:
        store.wait()


def fused(
    reps,
    tokens,
    routes,
    route_weight,
    w_gate,
    w_up,
    w_down,
    pseudo_grad,
    global_params,
    momentum,
    local_params,
):
    rows, width = tokens.shape
    experts, _, hidden = w_gate.shape
    frag_rows = momentum.shape[0]
    chips = reps // 2
    chunks, tiles = 2, 4
    f32, bf16 = jnp.float32, jnp.bfloat16
    anywhere = pl.BlockSpec(memory_space=pl.ANY)
    in_vmem = pl.BlockSpec(memory_space=pltpu.VMEM)
    dma = pltpu.SemaphoreType.DMA
    block = (frag_rows, LANES)
    returned = (chunks, tiles, rows // chunks, width // tiles)
    out_shape = (
        jax.ShapeDtypeStruct(tokens.shape, tokens.dtype),
        jax.ShapeDtypeStruct(momentum.shape, momentum.dtype),
        jax.ShapeDtypeStruct(local_params.shape, local_params.dtype),
    )
    results = pl.pallas_call(
        functools.partial(kernel, reps),
        out_shape=out_shape,
        in_specs=[anywhere, in_vmem, in_vmem] + [anywhere] * 7,
        out_specs=(anywhere,) * 3,
        scratch_shapes=[
            pltpu.VMEM((experts, width, 2 * hidden), bf16),
            pltpu.VMEM((experts * hidden, width), bf16),
            pltpu.VMEM((2 * rows, width), bf16),
            pltpu.VMEM((2 * rows, LANES), f32),
            pltpu.VMEM((8, rows), f32),
            pltpu.VMEM((8, rows), f32),
            pltpu.VMEM((2 * rows, experts * hidden), bf16),
            pltpu.VMEM((rows, width), f32),
            pltpu.VMEM(returned, bf16),
            pltpu.VMEM(returned, bf16),
            pltpu.VMEM(tokens.shape, bf16),
            pltpu.VMEM((chips,) + block, f32),
            pltpu.VMEM((chips,) + block, f32),
            pltpu.VMEM((chips,) + block, f32),
            pltpu.VMEM((chips,) + block, bf16),
            pltpu.VMEM((chips - 1,) + block, bf16),
            pltpu.VMEM((8, LANES), f32),
            pltpu.VMEM((chips - 1, 8, LANES), f32),
            pltpu.VMEM((8, LANES), f32),
            pltpu.VMEM((8, LANES), f32),
            pltpu.VMEM((8, LANES), f32),
            pltpu.VMEM((8, LANES), f32),
            pltpu.VMEM(block, f32),
            pltpu.VMEM(block, f32),
            pltpu.VMEM((frag_rows, width), f32),
            pltpu.VMEM((frag_rows, width), bf16),
            pltpu.VMEM((reps, 2) + block, bf16),
            pltpu.VMEM(block, f32),
            pltpu.VMEM((frag_rows, width), bf16),
            dma((experts, 2 * hidden // STRIP)),
            dma((experts,)),
            dma((4,)),
            dma((2 + chunks,)),
            dma((chips,)),
            dma((2, chunks)),
            dma((2, 1)),
            dma((2, chunks, tiles)),
            dma((2, chips)),
            dma((2, chips - 1)),
            dma((2, chips - 1)),
            dma((2, 2)),
            dma((2, chips - 1)),
            dma((2, chips - 1)),
            dma((2, chips // 2)),
            dma((2, chips)),
        ],
        compiler_params=pltpu.CompilerParams(
            collective_id=0, has_side_effects=True, vmem_limit_bytes=56 * 1024 * 1024
        ),
        cost_estimate=pl.CostEstimate(
            flops=12 * rows * experts * hidden * width,
            bytes_accessed=6 * experts * hidden * width,
            transcendentals=0,
        ),
    )(
        tokens,
        routes.T,
        route_weight.T,
        w_gate,
        w_up,
        w_down,
        pseudo_grad,
        global_params,
        momentum,
        local_params,
    )
    return pl.pallas_call(
        closing,
        out_shape=out_shape,
        in_specs=[anywhere] * 3,
        out_specs=(anywhere,) * 3,
        scratch_shapes=[
            pltpu.VMEM(tokens.shape, bf16),
            pltpu.VMEM(block, f32),
            pltpu.VMEM((frag_rows, width), bf16),
            dma((2, 5)),
        ],
        compiler_params=pltpu.CompilerParams(vmem_limit_bytes=60 * 1024 * 1024),
    )(*results)


def solution(mesh):
    in_specs = (
        P(("rep", "shard"), None),
        P(("rep", "shard"), None),
        P(("rep", "shard"), None),
        P("shard", None, None),
        P("shard", None, None),
        P("shard", None, None),
        P("rep", "shard", None),
        P("shard", None),
        P("shard", "rep"),
        P("rep", "shard", None),
    )
    out_specs = (P(("rep", "shard"), None), P("shard", "rep"), P("rep", "shard", None))
    reps, shards = mesh.shape["rep"], mesh.shape["shard"]

    def step(*arrays):
        tokens, w_gate, momentum = arrays[0], arrays[3], arrays[8]
        pairs = shards == 2 and reps % 4 == 0 and reps >= 8
        aligned = momentum.shape[1] == LANES and tokens.shape[0] == LANES
        if pairs and aligned and w_gate.shape[0] * shards == 8:
            return fused(reps, *arrays)
        return local(*arrays)

    return jax.shard_map(step, mesh=mesh, in_specs=in_specs, out_specs=out_specs, check_vma=False)
```
